128 devices in a mesh: gx: 16 (over z, x), gy: 2 (over y_lo), gz: 4 (over y_hi, core).
Axes of the slice: x: 4, y: 4 (y_hi: 2, y_lo: 2; y = y_hi * 2 + y_lo), z: 4, core: 2. Of those that a mesh axis runs over, the one named last changes fastest.
Arguments:
- tensor: float32 [512, 768, 512], P('gx', 'gy', 'gz'), may hold values from -12 to 12
- factor_b: float32 [768, 64], P(('gy', 'gx', 'gz')), may hold values from -8 to 8
- factor_c: float32 [512, 64], P(('gz', 'gx', 'gy')), may hold values from -8 to 8
Outputs:
- factor_a_out: float32 [512, 64], P(('gx', 'gy', 'gz'))
- factor_b_out: float32 [768, 64], P(('gy', 'gx', 'gz'))
- factor_c_out: float32 [512, 64], P(('gz', 'gx', 'gy'))
The draws below stay inside these ranges and needn't reach their ends.
All inputs are finite; a program needn't handle non-finite values.
Results may differ from the reference program's by a relative error of at most 0.0007.
Values sent between devices are 32-bit elements; how exact they have to be, the bound alone decides.
A program may use at most 64 MiB of HBM per device.

```python
import jax
import jax.numpy as jnp
from jax import lax

RANK = 64
SWEEPS = 1
EXTENT_I = 512
EXTENT_J = 768
EXTENT_K = 512


def mixed_columns(key, row_count):
    key_common, key_private = jax.random.split(key)
    common = jax.random.normal(key_common, (row_count, 1), jnp.float32)
    private = jax.random.normal(key_private, (row_count, RANK), jnp.float32)
    return 0.7 * common + 0.7 * private


def draw_tensor(key, part):
    key = jax.random.fold_in(key, 11)
    key_first, key_second, key_third, key_jitter = jax.random.split(key, 4)
    first = mixed_columns(key_first, EXTENT_I)
    second = mixed_columns(key_second, EXTENT_J)
    third = mixed_columns(key_third, EXTENT_K)
    paired = jnp.einsum('ir,jr->ijr', first, second)
    signal = jnp.einsum('ijr,kr->ijk', paired, third) / jnp.sqrt(jnp.float32(RANK))
    jitter = jax.random.normal(key_jitter, (EXTENT_I, EXTENT_J, EXTENT_K), jnp.float32)
    return jnp.clip(signal + 0.6 * jitter, -12.0, 12.0)


def factor_rows(key, row_count):
    key_common, key_private = jax.random.split(key, 2)
    common = jax.random.normal(key_common, (row_count, 1), jnp.float32)
    private = jax.random.normal(key_private, (row_count, RANK), jnp.float32)
    values = 0.7 * common + 0.7 * private
    return jnp.clip(values, -8.0, 8.0)


def draw_factor_b(key, part):
    key = jax.random.fold_in(key, 23)
    return factor_rows(key, EXTENT_J)


def draw_factor_c(key, part):
    key = jax.random.fold_in(key, 37)
    return factor_rows(key, EXTENT_K)


def setup_inputs(seed: int = 0) -> dict:
    seeds = jax.random.split(jax.random.key(seed), 4)
    return {
        "tensor": draw_tensor(jax.random.fold_in(seeds[3], 71), 0),
        "factor_b": draw_factor_b(jax.random.fold_in(seeds[3], 71), 0),
        "factor_c": draw_factor_c(jax.random.fold_in(seeds[3], 71), 0),
    }


HIGHEST_PRECISION = lax.Precision.HIGHEST

def solve_rows(moment, system):
    lower = jnp.linalg.cholesky(system)
    halfway = lax.linalg.triangular_solve(lower, moment, left_side=False, lower=True, transpose_a=True)
    return lax.linalg.triangular_solve(lower, halfway, left_side=False, lower=True, transpose_a=False)

def settle(unscaled, gram_raw, total_rows):
    scales = jnp.sqrt(jnp.diagonal(gram_raw) / total_rows + 1e-06)
    return (unscaled / scales[None, :], gram_raw / (scales[:, None] * scales[None, :]))

def gram_of(factor):
    return jnp.dot(factor.T.astype(jnp.float32), factor.astype(jnp.float32), precision=HIGHEST_PRECISION, preferred_element_type=jnp.float32)

def reference(tensor, factor_b, factor_c):
    current_b = factor_b
    current_c = factor_c
    gram_b = gram_of(current_b)
    gram_c = gram_of(current_c)
    current_a = jnp.zeros((EXTENT_I, RANK), jnp.float32)
    for sweep_no in range(SWEEPS):
        along_k = jnp.einsum('ijk,kr->rij', tensor, current_c, precision=HIGHEST_PRECISION)
        moment = jnp.einsum('rij,jr->ir', along_k, current_b, precision=HIGHEST_PRECISION)
        unscaled = solve_rows(moment, gram_b * gram_c)
        current_a, gram_a = settle(unscaled, gram_of(unscaled), EXTENT_I)
        moment = jnp.einsum('rij,ir->jr', along_k, current_a, precision=HIGHEST_PRECISION)
        unscaled = solve_rows(moment, gram_a * gram_c)
        current_b, gram_b = settle(unscaled, gram_of(unscaled), EXTENT_J)
        along_j = jnp.einsum('ijk,ir->rjk', tensor, current_a, precision=HIGHEST_PRECISION)
        moment = jnp.einsum('rjk,jr->kr', along_j, current_b, precision=HIGHEST_PRECISION)
        unscaled = solve_rows(moment, gram_a * gram_b)
        current_c, gram_c = settle(unscaled, gram_of(unscaled), EXTENT_K)
    return (current_a, current_b, current_c)
```

```python
import jax
import jax.numpy as jnp
from jax import lax
from jax.experimental import pallas as pl
from jax.experimental.pallas import tpu as pltpu
from jax.sharding import PartitionSpec as P

MESH = pl.DeviceIdType.MESH
HIGHEST = lax.Precision.HIGHEST
F32 = jnp.float32
BF16 = jnp.bfloat16

RANK = 64
GROUP = 4


def low(shape):
    return lax.broadcasted_iota(jnp.int32, shape, 1) < RANK


def swap(x):
    return pltpu.roll(x, RANK, 1)


def fold(x):
    return x + swap(x)


def compact(x):
    half = x.shape[0] // 2
    return jnp.where(low((half, 128)), x[:half], x[half:])


def expand(x):
    other = swap(x)
    side = low(x.shape)
    return jnp.concatenate([jnp.where(side, x, other), jnp.where(side, other, x)], axis=0)


def block_diagonal(x):
    side = low(x.shape)
    return jnp.concatenate([jnp.where(side, x, 0.0), jnp.where(side, 0.0, x)], axis=0)


def matmul(a, b):
    return jnp.dot(a, b, precision=HIGHEST, preferred_element_type=F32)


def gram_packed(x):
    full = matmul(x.T, x)
    own = jnp.where(low((RANK, 128)), full[:RANK] + swap(full[RANK:]), 0.0)
    return fold(own)


def scale_rows(gram, rows):
    r = lax.broadcasted_iota(jnp.int32, (RANK, 128), 0)
    c = lax.broadcasted_iota(jnp.int32, (RANK, 128), 1)
    both = jnp.where((c == r) | (c == r + RANK), gram, 0.0)
    across = jnp.sum(both, axis=0, keepdims=True)
    down = jnp.sum(jnp.where(c < RANK, both, 0.0), axis=1, keepdims=True)
    return jnp.sqrt(across / rows + 1e-06), jnp.sqrt(down / rows + 1e-06)


def inverse(system):
    lane = lax.broadcasted_iota(jnp.int32, (8, 128), 1) % RANK
    row = lax.broadcasted_iota(jnp.int32, (8, 128), 0)
    rest_lane = lax.broadcasted_iota(jnp.int32, (RANK - 8, 128), 1) % RANK

    def step(_, v):
        cols = [jnp.broadcast_to(v[:, c : c + 1], (RANK, 128)) for c in range(8)]
        diag = [col[:8] for col in cols]
        top = jnp.where(lane < 8, jnp.where(lane == row, 1.0, 0.0), v[:8])
        for c in range(8):
            pivot = 1.0 / jnp.broadcast_to(diag[c][c : c + 1], (8, 128))
            here = row == c
            factor = diag[c]
            line = jnp.broadcast_to(top[c : c + 1], (8, 128)) * pivot
            top = jnp.where(here, line, top - factor * line)
            for d in range(c + 1, 8):
                line = jnp.broadcast_to(diag[d][c : c + 1], (8, 128)) * pivot
                diag[d] = jnp.where(here, line, diag[d] - factor * line)
        rest = jnp.where(rest_lane < 8, 0.0, v[8:])
        for c in range(8):
            rest = rest - cols[c][8:] * jnp.broadcast_to(top[c : c + 1], (RANK - 8, 128))
        return pltpu.roll(jnp.concatenate([rest, top], axis=0), 128 - 8, 1)

    return lax.fori_loop(0, 8, step, system)


def split(x):
    high = x.astype(BF16)
    return high, (x - high.astype(F32)).astype(BF16)


def kernel(
    t_ref, fb_ref, fc_ref, a_ref, b_ref, c_ref,
    t32, thi, tlo, along, weights,
    c_one, c_all, b_one, b_all, b_packed,
    gb_slots, gc_slots, ma_part, ma_slots, ua_slots, ua_rows, a_columns,
    mb_part, mb_slots, mb_sum, ub, gu_slots, mc_part, mc_slots, mc_sum, ss_slots,
    t_sem, send, recv,
):
    gx, gy, gz = lax.axis_index("gx"), lax.axis_index("gy"), lax.axis_index("gz")
    z, x = gx // 4, lax.rem(gx, 4)
    yh, core = gz // 2, lax.rem(gz, 2)
    span_i = t_ref.shape[0]

    def ring(me, size, place):
        return me, [place(lax.rem(me + d, size)) for d in range(1, size)]

    gy_me, gy_peers = ring(gy, 2, lambda p: (gx, p, gz))
    gz_me, gz_peers = ring(gz, 4, lambda p: (gx, gy, p))
    gx_me, gx_peers = ring(gx, 16, lambda p: (p, gy, gz))
    yc_me, yc_peers = ring(gy * 4 + gz, 8, lambda p: (gx, p // 4, lax.rem(p, 4)))
    xc_me, xc_peers = ring(x * 2 + core, 8, lambda p: (z * 4 + p // 2, gy, yh * 2 + lax.rem(p, 2)))
    zh_me, zh_peers = ring(z * 2 + yh, 8, lambda p: ((p // 2) * 4 + x, gy, lax.rem(p, 2) * 2 + core))
    xx_me, xx_peers = ring(x, 4, lambda p: (z * 4 + p, gy, gz))
    zl_me, zl_peers = ring(z * 2 + gy, 8, lambda p: ((p // 2) * 4 + x, lax.rem(p, 2), gz))
    xg_me, xg_peers = ring(x * 4 + gz, 16, lambda p: (z * 4 + p // 4, gy, lax.rem(p, 4)))

    pending = []
    used = [0]

    def start(peers, source, target):
        copies = []
        for d, peer in enumerate(peers):
            at = used[0]
            used[0] += 1
            copy = pltpu.make_async_remote_copy(
                src_ref=source(d + 1),
                dst_ref=target,
                send_sem=send.at[at],
                recv_sem=recv.at[at],
                device_id=peer,
                device_id_type=MESH,
            )
            copy.start()
            copies.append(copy)
        pending.extend(copies)
        return copies

    def arrive(copies):
        for copy in copies:
            copy.wait_recv()

    for q in range(span_i // GROUP):
        pltpu.make_async_copy(
            t_ref.at[pl.ds(q * GROUP, GROUP)], t32.at[pl.ds(q * GROUP, GROUP)], t_sem.at[q]
        ).start()

    barrier = pltpu.get_barrier_semaphore()
    greeted = gx_peers + yc_peers
    for peer in greeted:
        pl.semaphore_signal(barrier, inc=1, device_id=peer, device_id_type=MESH)

    c_one[gy] = jnp.concatenate([fc_ref[...], fc_ref[...]], axis=1)
    b_one[gz] = jnp.concatenate([fb_ref[...], fb_ref[...]], axis=1)

    def split_tensor(q, _):
        rows = pl.ds(q * GROUP, GROUP)
        pltpu.make_async_copy(t_ref.at[rows], t32.at[rows], t_sem.at[q]).wait()

        def one(i, _):
            thi[i], tlo[i] = split(t32[i])
            return 0

        lax.fori_loop(q * GROUP, (q + 1) * GROUP, one, 0)
        return 0

    pl.semaphore_wait(barrier, len(greeted))

    c_first = start(gy_peers, lambda d: c_one.at[gy], c_one.at[gy])
    b_first = start(gz_peers, lambda d: b_one.at[gz], b_one.at[gz])
    lax.fori_loop(0, 2, split_tensor, 0)
    arrive(c_first)
    c_all[gx] = jnp.where(low((4, 128)), c_one[0], c_one[1])
    c_second = start(gx_peers, lambda d: c_all.at[gx], c_all.at[gx])
    arrive(b_first)
    b_all[gx] = jnp.concatenate(
        [jnp.where(low((6, 128)), b_one[0], b_one[2]), jnp.where(low((6, 128)), b_one[1], b_one[3])],
        axis=0,
    )
    b_second = start(gx_peers, lambda d: b_all.at[gx], b_all.at[gx])
    lax.fori_loop(2, span_i // GROUP, split_tensor, 0)

    arrive(c_second)
    pieces = []
    for g in range(16):
        piece = c_all[g]
        other = swap(piece)
        side = low((4, 128))
        pieces += [jnp.where(side, piece, other), jnp.where(side, other, piece)]
    block_c = jnp.concatenate(pieces, axis=0)
    gram_c = matmul(block_c.T, block_c)[:RANK]
    gc_slots[gz] = compact(gram_c)
    gc_copies = start(gz_peers, lambda d: gc_slots.at[gz], gc_slots.at[gz])
    c_high, c_low = split(block_c)
    side = low((128, 128))
    none = jnp.zeros((128, 128), BF16)
    weights[:128, :128] = jnp.where(side, c_high, none)
    weights[:128, 128:] = jnp.where(side, c_low, none)
    weights[128:, :128] = jnp.where(side, none, c_high)
    weights[128:, 128:] = jnp.where(side, none, c_low)

    half_j = along.shape[1]

    def along_step(q, _):
        rows = pl.ds(q * GROUP, GROUP)

        def wide(ref):
            left, right = ref[rows, :half_j, :], ref[rows, half_j:, :]
            return jnp.concatenate([left, right], axis=2).reshape(GROUP * half_j, 256)

        both = jnp.dot(wide(thi), weights[...], preferred_element_type=F32)
        rest = jnp.dot(wide(tlo), weights[:, :128], preferred_element_type=F32)
        total = both[:, :128] + (both[:, 128:] + rest)
        along[rows] = total.reshape(GROUP, half_j, 128)
        return 0

    lax.fori_loop(0, span_i // GROUP, along_step, 0)

    arrive(b_second)
    for g in range(8):
        one, two = b_all[g], b_all[g + 8]
        side = low((12, 128))
        b_packed[24 * g : 24 * g + 12, :] = jnp.where(side, one, swap(two))
        b_packed[24 * g + 12 : 24 * g + 24, :] = jnp.where(side, swap(one), two)
    block_b = b_packed[...]

    def moment_a(i, _):
        product = along[i] * block_b
        ma_part[i] = jnp.sum(product.reshape(half_j // 8, 8, 128), axis=0)
        return 0

    lax.fori_loop(0, span_i, moment_a, 0)
    ma_slots[yc_me] = compact(fold(jnp.sum(ma_part[...], axis=1)))
    ma_copies = start(yc_peers, lambda d: ma_slots.at[yc_me], ma_slots.at[yc_me])
    gb_slots[gy] = compact(gram_packed(block_b))
    gb_copies = start(gy_peers, lambda d: gb_slots.at[gy], gb_slots.at[gy])
    arrive(gc_copies)
    arrive(gb_copies)
    gram_c = expand(gc_slots[0] + gc_slots[1] + gc_slots[2] + gc_slots[3])
    gram_b = expand(gb_slots[0] + gb_slots[1])
    inverse_a = block_diagonal(inverse(gram_b * gram_c))
    arrive(ma_copies)
    moment = ma_slots[0]
    for g in range(1, 8):
        moment = moment + ma_slots[g]
    ua = matmul(moment, inverse_a)
    ua_slots[gx] = ua
    ua_copies = start(gx_peers, lambda d: ua_slots.at[gx], ua_slots.at[gx])

    ua_rows[...] = expand(ua)

    def moment_b(i, total):
        return total + along[i] * ua_rows[pl.ds(i, 1), :]

    moment = lax.fori_loop(0, span_i, moment_b, jnp.zeros((half_j, 128), F32), unroll=4)
    mb_part[...] = moment.reshape(mb_part.shape)
    mb_slots[xc_me] = mb_part[xc_me]
    mb_copies = start(xc_peers, lambda d: mb_part.at[lax.rem(xc_me + d, 8)], mb_slots.at[xc_me])
    arrive(mb_copies)
    moment = mb_slots[0]
    for g in range(1, 8):
        moment = moment + mb_slots[g]
    mb_sum[zh_me] = moment
    mb_copies = start(zh_peers, lambda d: mb_sum.at[zh_me], mb_sum.at[zh_me])
    arrive(ua_copies)
    gram_ua = gram_packed(ua_slots[...].reshape(256, 128))
    scale_a, scale_a_down = scale_rows(gram_ua, float(span_i * 16))
    gram_a = gram_ua / (scale_a * scale_a_down)
    inverse_b = block_diagonal(inverse(gram_a * gram_c))
    shard_a = ua_slots[gx] / scale_a
    full_a = expand(shard_a)
    turned = jnp.concatenate([full_a, full_a, full_a, full_a], axis=0).T
    for i in range(32):
        a_columns[i] = jnp.broadcast_to(turned[:RANK, i : i + 1], (RANK, 128))
    picked = jnp.where(gy == 0, shard_a, swap(shard_a))
    ua_rows[:16, :] = picked
    a_ref[...] = ua_rows[pl.ds(gz * 4, 4), :][:, :RANK]
    arrive(mb_copies)
    moment = mb_sum[0]
    for g in range(1, 8):
        moment = moment + mb_sum[g]
    ub[xc_me] = matmul(moment / scale_a, inverse_b)
    ub_copies = start(xc_peers, lambda d: ub.at[xc_me], ub.at[xc_me])
    arrive(ub_copies)

    block_b = ub[...].reshape(half_j, 128)
    gu_slots[gy] = compact(gram_packed(block_b))
    gu_copies = start(gy_peers, lambda d: gu_slots.at[gy], gu_slots.at[gy])
    turned = block_b.T
    turned_high, turned_low = split(turned)
    left = [
        jnp.concatenate([turned_high[h * RANK : (h + 1) * RANK], turned_low[h * RANK : (h + 1) * RANK]], axis=0)
        for h in range(2)
    ]
    left = jnp.concatenate(left, axis=1)

    def moment_c(i, total):
        right = jnp.concatenate([thi[i], tlo[i]], axis=1)
        part = jnp.dot(left, right, preferred_element_type=F32)
        part = part[:RANK, :128] + (part[:RANK, 128:] + part[RANK:, :128])
        return total + part * a_columns[i]

    moment = lax.fori_loop(0, span_i, moment_c, jnp.zeros((RANK, 128), F32), unroll=2)
    moment = compact(jnp.concatenate([moment, moment], axis=0).T)
    for p in range(4):
        mc_part[p, :8, :] = moment[p * 8 : p * 8 + 8]
        mc_part[p, 8:, :] = moment[32 + p * 8 : 32 + p * 8 + 8]
    mc_slots[x] = mc_part[x]
    mc_copies = start(xx_peers, lambda d: mc_part.at[lax.rem(x + d, 4)], mc_slots.at[x])
    arrive(gu_copies)
    gram_ub = expand(gu_slots[0] + gu_slots[1])
    scale_b, scale_b_down = scale_rows(gram_ub, float(half_j * 4))
    gram_b = gram_ub / (scale_b * scale_b_down)
    arrive(mc_copies)
    mc_sum[zl_me] = mc_slots[0] + mc_slots[1] + (mc_slots[2] + mc_slots[3])
    mc_copies = start(zl_peers, lambda d: mc_sum.at[zl_me], mc_sum.at[zl_me])
    inverse_c = block_diagonal(inverse(gram_a * gram_b))
    shard_b = block_b / scale_b
    b_packed[...] = jnp.where(z // 2 == 0, shard_b, swap(shard_b))
    first = lax.rem(z, 2) * 96 + x * 24 + yh * 12 + core * 6
    b_ref[...] = b_packed[pl.ds(first, 6), :][:, :RANK]
    arrive(mc_copies)
    moment = mc_sum[0]
    for g in range(1, 8):
        moment = moment + mc_sum[g]
    uc = matmul(moment / scale_b, inverse_c)
    ss_slots[xg_me] = fold(jnp.sum(uc * uc, axis=0, keepdims=True))
    ss_copies = start(xg_peers, lambda d: ss_slots.at[xg_me], ss_slots.at[xg_me])
    picked = jnp.where(z // 2 == 0, uc, swap(uc))
    arrive(ss_copies)
    total = jnp.sum(ss_slots[...], axis=0)
    scale_c = jnp.sqrt(total / float(128 * 4) + 1e-06)
    ua_rows[:16, :] = picked / scale_c
    c_ref[...] = ua_rows[pl.ds(lax.rem(z, 2) * 8 + gy * 4, 4), :][:, :RANK]

    for copy in pending:
        copy.wait_send()


COPIES = 1 + 3 + 15 + 15 + 3 + 7 + 1 + 15 + 7 + 7 + 7 + 1 + 3 + 7 + 15


def local(tensor, factor_b, factor_c):
    span_i, span_j, span_k = tensor.shape
    half_j = span_j // 2
    vmem = pl.BlockSpec(memory_space=pltpu.VMEM)
    scratch = [
        pltpu.VMEM(tensor.shape, F32),
        pltpu.VMEM(tensor.shape, BF16),
        pltpu.VMEM(tensor.shape, BF16),
        pltpu.VMEM((span_i, half_j, 128), F32),
        pltpu.VMEM((256, 256), BF16),
        pltpu.VMEM((2, 4, 128), F32),
        pltpu.VMEM((16, 4, 128), F32),
        pltpu.VMEM((4, 6, 128), F32),
        pltpu.VMEM((16, 12, 128), F32),
        pltpu.VMEM((half_j, 128), F32),
        pltpu.VMEM((2, 32, 128), F32),
        pltpu.VMEM((4, 32, 128), F32),
        pltpu.VMEM((span_i, 8, 128), F32),
        pltpu.VMEM((8, 16, 128), F32),
        pltpu.VMEM((16, 16, 128), F32),
        pltpu.VMEM((32, 128), F32),
        pltpu.VMEM((32, RANK, 128), F32),
        pltpu.VMEM((8, 24, 128), F32),
        pltpu.VMEM((8, 24, 128), F32),
        pltpu.VMEM((8, 24, 128), F32),
        pltpu.VMEM((8, 24, 128), F32),
        pltpu.VMEM((2, 32, 128), F32),
        pltpu.VMEM((4, 16, 128), F32),
        pltpu.VMEM((4, 16, 128), F32),
        pltpu.VMEM((8, 16, 128), F32),
        pltpu.VMEM((16, 1, 128), F32),
        pltpu.SemaphoreType.DMA((span_i // GROUP,)),
        pltpu.SemaphoreType.DMA((COPIES,)),
        pltpu.SemaphoreType.DMA((COPIES,)),
    ]
    return pl.pallas_call(
        kernel,
        out_shape=(
            jax.ShapeDtypeStruct((4, RANK), F32),
            jax.ShapeDtypeStruct((6, RANK), F32),
            jax.ShapeDtypeStruct((4, RANK), F32),
        ),
        in_specs=[pl.BlockSpec(memory_space=pl.ANY), vmem, vmem],
        out_specs=(vmem, vmem, vmem),
        scratch_shapes=scratch,
        compiler_params=pltpu.CompilerParams(
            collective_id=0, has_side_effects=True, vmem_limit_bytes=48 * 1024 * 1024
        ),
    )(tensor, factor_b, factor_c)


def solution(mesh):
    return jax.shard_map(
        local,
        mesh=mesh,
        in_specs=(P("gx", "gy", "gz"), P(("gy", "gx", "gz"), None), P(("gz", "gx", "gy"), None)),
        out_specs=(
            P(("gx", "gy", "gz"), None),
            P(("gy", "gx", "gz"), None),
            P(("gz", "gx", "gy"), None),
        ),
        check_vma=False,
    )
```

```python
import itertools

import jax
import jax.numpy as jnp
from jax import lax
from jax.experimental import pallas as pl
from jax.experimental.pallas import tpu as pltpu
from jax.sharding import PartitionSpec as P

MESH = pl.DeviceIdType.MESH
HIGHEST = lax.Precision.HIGHEST
F32 = jnp.float32
BF16 = jnp.bfloat16

RANK = 64
GROUP = 8
SIZES = {"z": 4, "x": 4, "yh": 2, "gy": 2, "core": 2}


def low(shape):
    return lax.broadcasted_iota(jnp.int32, shape, 1) < RANK


def swap(x):
    return pltpu.roll(x, RANK, 1)


def fold(x):
    return x + swap(x)


def compact(x):
    half = x.shape[0] // 2
    return jnp.where(low((half, 128)), x[:half], x[half:])


def expand(x):
    other = swap(x)
    side = low(x.shape)
    return jnp.concatenate([jnp.where(side, x, other), jnp.where(side, other, x)], axis=0)


def block_diagonal(x):
    side = low(x.shape)
    return jnp.concatenate([jnp.where(side, x, 0.0), jnp.where(side, 0.0, x)], axis=0)


def matmul(a, b):
    return jnp.dot(a, b, precision=HIGHEST, preferred_element_type=F32)


def gram_packed(x):
    full = matmul(x.T, x)
    own = jnp.where(low((RANK, 128)), full[:RANK] + swap(full[RANK:]), 0.0)
    return fold(own)


def scale_rows(gram, rows):
    r = lax.broadcasted_iota(jnp.int32, (RANK, 128), 0)
    c = lax.broadcasted_iota(jnp.int32, (RANK, 128), 1)
    both = jnp.where((c == r) | (c == r + RANK), gram, 0.0)
    across = jnp.sum(both, axis=0, keepdims=True)
    down = jnp.sum(jnp.where(c < RANK, both, 0.0), axis=1, keepdims=True)
    return jnp.sqrt(across / rows + 1e-06), jnp.sqrt(down / rows + 1e-06)


def inverse(system):
    lane = lax.broadcasted_iota(jnp.int32, (8, 128), 1) % RANK
    row = lax.broadcasted_iota(jnp.int32, (8, 128), 0)
    rest_lane = lax.broadcasted_iota(jnp.int32, (RANK - 8, 128), 1) % RANK

    def step(_, v):
        cols = [jnp.broadcast_to(v[:, c : c + 1], (RANK, 128)) for c in range(8)]
        diag = [col[:8] for col in cols]
        top = jnp.where(lane < 8, jnp.where(lane == row, 1.0, 0.0), v[:8])
        for c in range(8):
            pivot = 1.0 / jnp.broadcast_to(diag[c][c : c + 1], (8, 128))
            here = row == c
            factor = diag[c]
            line = jnp.broadcast_to(top[c : c + 1], (8, 128)) * pivot
            top = jnp.where(here, line, top - factor * line)
            for d in range(c + 1, 8):
                line = jnp.broadcast_to(diag[d][c : c + 1], (8, 128)) * pivot
                diag[d] = jnp.where(here, line, diag[d] - factor * line)
        rest = jnp.where(rest_lane < 8, 0.0, v[8:])
        for c in range(8):
            rest = rest - cols[c][8:] * jnp.broadcast_to(top[c : c + 1], (RANK - 8, 128))
        return pltpu.roll(jnp.concatenate([rest, top], axis=0), 128 - 8, 1)

    return lax.fori_loop(0, 8, step, system)


def split(x):
    high = x.astype(BF16)
    return high, (x - high.astype(F32)).astype(BF16)


def kernel(
    t_ref, start_ref, out_ref,
    t32, thi, tlo, along, weights,
    c_one, c_all, b_one, b_all, b_packed,
    gb_slots, gc_slots, ma_part, ma_slots, ua_slots, ua_rows, a_columns,
    mb_part, mb_slots, mb_sum, ub, gu_slots, mc_part, mc_slot, mc_sum, ss_slots, rows_out,
    t_sem, send, recv,
):
    gx, gy, gz = lax.axis_index("gx"), lax.axis_index("gy"), lax.axis_index("gz")
    z, x = gx // 4, lax.rem(gx, 4)
    yh, core = gz // 2, lax.rem(gz, 2)
    span_i = t_ref.shape[0]

    here = {"z": z, "x": x, "yh": yh, "gy": gy, "core": core}

    def group(*names):
        sizes = [SIZES[name] for name in names]

        def number(place):
            out = 0
            for name, size in zip(names, sizes):
                out = out * size + place[name]
            return out

        def hops(shift):
            shift = dict(zip(names, shift))
            y = 2 * shift.get("yh", 0) + shift.get("gy", 0)
            far = [min(n, 4 - n) for n in (shift.get("z", 0), shift.get("x", 0), y)]
            return sum(far) + 0.5 * shift.get("core", 0)

        shifts = sorted(itertools.product(*[range(size) for size in sizes]), key=hops, reverse=True)
        peers = []
        for shift in shifts[:-1]:
            place = dict(here)
            for name, size, n in zip(names, sizes, shift):
                if n:
                    place[name] = lax.rem(here[name] + n, size)
            device = (place["z"] * 4 + place["x"], place["gy"], place["yh"] * 2 + place["core"])
            peers.append((number(place), device))
        return number(here), peers

    gy_me, gy_peers = group("gy")
    gz_me, gz_peers = group("yh", "core")
    gx_me, gx_peers = group("z", "x")
    yc_me, yc_peers = group("gy", "yh", "core")
    xc_me, xc_peers = group("x", "core")
    zh_me, zh_peers = group("z", "yh")

    pending = []
    used = [0]

    def start_one(peer, source, target):
        at = used[0]
        used[0] += 1
        copy = pltpu.make_async_remote_copy(
            src_ref=source,
            dst_ref=target,
            send_sem=send.at[at],
            recv_sem=recv.at[at],
            device_id=peer[1],
            device_id_type=MESH,
        )
        copy.start()
        pending.append(copy)
        return copy

    def start(peers, source, target):
        return [start_one(peer, source, target) for peer in peers]

    def arrive(copies):
        for copy in copies:
            copy.wait_recv()

    def drain(keep=0):
        while len(pending) > keep:
            pending.pop(0).wait_send()

    barrier = pltpu.get_barrier_semaphore()
    greeted = gx_peers + yc_peers
    for peer in greeted:
        pl.semaphore_signal(barrier, inc=1, device_id=peer[1], device_id_type=MESH)
    c_one[gy] = start_ref[8:, :]
    b_one[gz] = start_ref[:8, :]

    def load(q):
        rows = pl.ds(q * GROUP, GROUP)
        return pltpu.make_async_copy(t_ref.at[rows], t32.at[rows], t_sem.at[q])

    def split_tensor(q, _):
        load(q).wait()

        def one(i, _):
            thi[i], tlo[i] = split(t32[i])
            return 0

        lax.fori_loop(q * GROUP, (q + 1) * GROUP, one, 0)
        return 0

    pl.semaphore_wait(barrier, len(greeted))

    c_first = start(gy_peers, start_ref.at[pl.ds(8, 8)], c_one.at[gy])
    b_first = start(gz_peers, start_ref.at[pl.ds(0, 8)], b_one.at[gz])
    for q in range(span_i // GROUP):
        load(q).start()
    arrive(c_first)
    c_all[gx] = jnp.concatenate([c_one[0][:4], c_one[1][:4]], axis=1)
    c_second = start(gx_peers, c_all.at[gx], c_all.at[gx])
    arrive(b_first)
    b_all[gx] = jnp.concatenate(
        [
            jnp.concatenate([b_one[0][:6], b_one[2][:6]], axis=1),
            jnp.concatenate([b_one[1][:6], b_one[3][:6]], axis=1),
        ],
        axis=0,
    )
    b_second = start(gx_peers, b_all.at[gx], b_all.at[gx])
    lax.fori_loop(0, span_i // GROUP, split_tensor, 0)
    drain(30)
    arrive(c_second)
    pieces = []
    for g in range(16):
        piece = c_all[g]
        other = swap(piece)
        side = low((4, 128))
        pieces += [jnp.where(side, piece, other), jnp.where(side, other, piece)]
    block_c = jnp.concatenate(pieces, axis=0)
    gram_c = matmul(block_c.T, block_c)[:RANK]
    gc_slots[gz] = compact(gram_c)
    gc_copies = start(gz_peers, gc_slots.at[gz], gc_slots.at[gz])
    c_high, c_low = split(block_c)
    side = low((128, 128))
    none = jnp.zeros((128, 128), BF16)
    weights[:128, :128] = jnp.where(side, c_high, none)
    weights[:128, 128:] = jnp.where(side, c_low, none)
    weights[128:, :128] = jnp.where(side, none, c_high)
    weights[128:, 128:] = jnp.where(side, none, c_low)

    half_j = along.shape[1]

    def along_step(q, _):
        rows = pl.ds(q * GROUP, GROUP)

        def wide(ref):
            left, right = ref[rows, :half_j, :], ref[rows, half_j:, :]
            return jnp.concatenate([left, right], axis=2).reshape(GROUP * half_j, 256)

        both = jnp.dot(wide(thi), weights[...], preferred_element_type=F32)
        rest = jnp.dot(wide(tlo), weights[:, :128], preferred_element_type=F32)
        total = both[:, :128] + (both[:, 128:] + rest)
        along[rows] = total.reshape(GROUP, half_j, 128)
        return 0

    steps = span_i // GROUP
    lax.fori_loop(0, steps // 2, along_step, 0)
    arrive(b_second)
    for g in range(8):
        one, two = b_all[g], b_all[g + 8]
        side = low((12, 128))
        b_packed[24 * g : 24 * g + 12, :] = jnp.where(side, one, swap(two))
        b_packed[24 * g + 12 : 24 * g + 24, :] = jnp.where(side, swap(one), two)
    block_b = b_packed[...]
    gb_slots[gy] = compact(gram_packed(block_b))
    gb_copies = start(gy_peers, gb_slots.at[gy], gb_slots.at[gy])
    lax.fori_loop(steps // 2, steps, along_step, 0)
    def moment_a(i, _):
        product = along[i] * block_b
        ma_part[i] = jnp.sum(product.reshape(half_j // 8, 8, 128), axis=0)
        return 0

    lax.fori_loop(0, span_i, moment_a, 0)
    ma_slots[yc_me] = compact(fold(jnp.sum(ma_part[...], axis=1)))
    ma_copies = start(yc_peers, ma_slots.at[yc_me], ma_slots.at[yc_me])
    drain(7)
    arrive(gc_copies)
    arrive(gb_copies)
    gram_c = expand(gc_slots[0] + gc_slots[1] + gc_slots[2] + gc_slots[3])
    gram_b = expand(gb_slots[0] + gb_slots[1])
    inverse_a = block_diagonal(inverse(gram_b * gram_c))
    arrive(ma_copies)
    moment = ma_slots[0]
    for g in range(1, 8):
        moment = moment + ma_slots[g]
    ua = matmul(moment, inverse_a)
    ua_slots[gx] = ua
    rows_a = expand(ua)
    for i in range(32):
        ua_rows[i] = jnp.broadcast_to(rows_a[i : i + 1], (8, 128))

    def moment_b(chunk):
        rows = pl.ds(pl.multiple_of(chunk * 24, 8), 24)
        total = jnp.zeros((3, 8, 128), F32)
        for q in range(4):
            some = along[8 * q : 8 * q + 8, rows, :].reshape(8, 3, 8, 128)
            total = total + jnp.sum(some * ua_rows[8 * q : 8 * q + 8][:, None], axis=0)
        return total.reshape(24, 128)

    mb_copies = []
    for peer in xc_peers:
        mb_part[peer[0]] = moment_b(peer[0])
        mb_copies.append(start_one(peer, mb_part.at[peer[0]], mb_slots.at[xc_me]))
    mb_slots[xc_me] = moment_b(xc_me)
    ua_copies = start(gx_peers, ua_slots.at[gx], ua_slots.at[gx])
    drain(22)
    arrive(mb_copies)
    moment = mb_slots[0]
    for g in range(1, 8):
        moment = moment + mb_slots[g]
    mb_sum[zh_me] = moment
    mb_copies = start(zh_peers, mb_sum.at[zh_me], mb_sum.at[zh_me])
    arrive(ua_copies)
    gram_ua = gram_packed(ua_slots[...].reshape(256, 128))
    scale_a, scale_a_down = scale_rows(gram_ua, float(span_i * 16))
    gram_a = gram_ua / (scale_a * scale_a_down)
    inverse_b = block_diagonal(inverse(gram_a * gram_c))
    shard_a = ua_slots[gx] / scale_a
    full_a = expand(shard_a)
    turned = jnp.concatenate([full_a, full_a, full_a, full_a], axis=0).T
    for i in range(32):
        a_columns[i] = jnp.broadcast_to(turned[:RANK, i : i + 1], (RANK, 128))
    rows_out[:16, :] = jnp.where(gy == 0, shard_a, swap(shard_a))
    out_ref[:4, :] = rows_out[pl.ds(gz * 4, 4), :]
    drain(7)
    arrive(mb_copies)
    moment = mb_sum[0]
    for g in range(1, 8):
        moment = moment + mb_sum[g]
    ub[xc_me] = matmul(moment / scale_a, inverse_b)
    ub_copies = start(xc_peers, ub.at[xc_me], ub.at[xc_me])
    drain(7)
    arrive(ub_copies)

    block_b = ub[...].reshape(half_j, 128)
    turned = block_b.T
    turned_high, turned_low = split(turned)
    left = [
        jnp.concatenate([turned_high[h * RANK : (h + 1) * RANK], turned_low[h * RANK : (h + 1) * RANK]], axis=0)
        for h in range(2)
    ]
    left = jnp.concatenate(left, axis=1)

    def moment_c(i, total):
        right = jnp.concatenate([thi[i], tlo[i]], axis=1)
        part = jnp.dot(left, right, preferred_element_type=F32)
        part = part[:RANK, :128] + (part[:RANK, 128:] + part[RANK:, :128])
        return total + part * a_columns[i]

    moment = lax.fori_loop(0, span_i, moment_c, jnp.zeros((RANK, 128), F32), unroll=4)
    moment = compact(jnp.concatenate([moment, moment], axis=0).T)
    upper = lax.broadcasted_iota(jnp.int32, (8, 128), 0) < 4
    parts = [[], []]
    for m in range(4):
        one, two = moment[16 * m : 16 * m + 8], moment[16 * m + 8 : 16 * m + 16]
        parts[0].append(jnp.where(upper, one, pltpu.roll(two, 4, 0)))
        parts[1].append(jnp.where(upper, pltpu.roll(one, 4, 0), two))
    parts = [jnp.concatenate(part, axis=0) for part in parts]
    mc_part[...] = jnp.where(gy == 0, parts[1], parts[0])
    mc_copies = start(gy_peers, mc_part, mc_slot)
    gu_slots[gy] = compact(gram_packed(block_b))
    gu_copies = start(gy_peers, gu_slots.at[gy], gu_slots.at[gy])
    drain(2)
    arrive(mc_copies)
    mc_sum[gx] = jnp.where(gy == 0, parts[0], parts[1]) + mc_slot[...]
    mc_copies = start(gx_peers, mc_sum.at[gx], mc_sum.at[gx])
    arrive(gu_copies)
    gram_ub = expand(gu_slots[0] + gu_slots[1])
    scale_b, scale_b_down = scale_rows(gram_ub, float(half_j * 4))
    gram_b = gram_ub / (scale_b * scale_b_down)
    inverse_c = block_diagonal(inverse(gram_a * gram_b))
    shard_b = block_b / scale_b
    b_packed[...] = jnp.where(z // 2 == 0, shard_b, swap(shard_b))
    first = lax.rem(z, 2) * 96 + x * 24 + yh * 12 + core * 6
    out_ref[8:14, :] = b_packed[pl.ds(first, 6), :]
    drain(15)
    arrive(mc_copies)
    moment = mc_sum[0]
    for g in range(1, 16):
        moment = moment + mc_sum[g]
    uc = matmul(moment / scale_b, inverse_c)
    ss_slots[yc_me] = fold(jnp.sum(uc * uc, axis=0, keepdims=True))
    ss_copies = start(yc_peers, ss_slots.at[yc_me], ss_slots.at[yc_me])
    drain(7)
    arrive(ss_copies)
    total = jnp.sum(ss_slots[...], axis=0)
    scale_c = jnp.sqrt(total / float(128 * 4) + 1e-06)
    rows_out[...] = jnp.where(z // 2 == 0, uc, swap(uc)) / scale_c
    out_ref[4:8, :] = rows_out[pl.ds(lax.rem(gx, 8) * 4, 4), :]
    drain()


COPIES = 1 + 3 + 15 + 15 + 3 + 1 + 7 + 7 + 15 + 7 + 7 + 1 + 1 + 15 + 7


def local(tensor, factor_b, factor_c):
    span_i, span_j, span_k = tensor.shape
    half_j = span_j // 2
    vmem = pl.BlockSpec(memory_space=pltpu.VMEM)
    scratch = [
        pltpu.VMEM(tensor.shape, F32),
        pltpu.VMEM(tensor.shape, BF16),
        pltpu.VMEM(tensor.shape, BF16),
        pltpu.VMEM((span_i, half_j, 128), F32),
        pltpu.VMEM((256, 256), BF16),
        pltpu.VMEM((2, 8, RANK), F32),
        pltpu.VMEM((16, 4, 128), F32),
        pltpu.VMEM((4, 8, RANK), F32),
        pltpu.VMEM((16, 12, 128), F32),
        pltpu.VMEM((half_j, 128), F32),
        pltpu.VMEM((2, 32, 128), F32),
        pltpu.VMEM((4, 32, 128), F32),
        pltpu.VMEM((span_i, 8, 128), F32),
        pltpu.VMEM((8, 16, 128), F32),
        pltpu.VMEM((16, 16, 128), F32),
        pltpu.VMEM((32, 8, 128), F32),
        pltpu.VMEM((32, RANK, 128), F32),
        pltpu.VMEM((8, 24, 128), F32),
        pltpu.VMEM((8, 24, 128), F32),
        pltpu.VMEM((8, 24, 128), F32),
        pltpu.VMEM((8, 24, 128), F32),
        pltpu.VMEM((2, 32, 128), F32),
        pltpu.VMEM((32, 128), F32),
        pltpu.VMEM((32, 128), F32),
        pltpu.VMEM((16, 32, 128), F32),
        pltpu.VMEM((8, 1, 128), F32),
        pltpu.VMEM((32, 128), F32),
        pltpu.SemaphoreType.DMA((span_i // GROUP,)),
        pltpu.SemaphoreType.DMA((COPIES,)),
        pltpu.SemaphoreType.DMA((COPIES,)),
    ]
    start = jnp.concatenate(
        [jnp.pad(factor_b, ((0, 2), (0, 0))), jnp.pad(factor_c, ((0, 4), (0, 0)))], axis=0
    )
    out = pl.pallas_call(
        kernel,
        out_shape=jax.ShapeDtypeStruct((16, 128), F32),
        in_specs=[pl.BlockSpec(memory_space=pl.ANY), vmem],
        out_specs=vmem,
        scratch_shapes=scratch,
        compiler_params=pltpu.CompilerParams(
            collective_id=0, has_side_effects=True, vmem_limit_bytes=48 * 1024 * 1024
        ),
    )(tensor, start)
    return out[:4, :RANK], out[8:14, :RANK], out[4:8, :RANK]


def solution(mesh):
    return jax.shard_map(
        local,
        mesh=mesh,
        in_specs=(P("gx", "gy", "gz"), P(("gy", "gx", "gz"), None), P(("gz", "gx", "gy"), None)),
        out_specs=(
            P(("gx", "gy", "gz"), None),
            P(("gy", "gx", "gz"), None),
            P(("gz", "gx", "gy"), None),
        ),
        check_vma=False,
    )
```

```python
import itertools

import jax
import jax.numpy as jnp
from jax import lax
from jax.experimental import pallas as pl
from jax.experimental.pallas import tpu as pltpu
from jax.sharding import PartitionSpec as P

MESH = pl.DeviceIdType.MESH
HIGHEST = lax.Precision.HIGHEST
F32 = jnp.float32
BF16 = jnp.bfloat16

RANK = 64
GROUP = 8
SIZES = {"z": 4, "x": 4, "yh": 2, "gy": 2, "core": 2}


def low(shape):
    return lax.broadcasted_iota(jnp.int32, shape, 1) < RANK


def swap(x):
    return pltpu.roll(x, RANK, 1)


def fold(x):
    return x + swap(x)


def compact(x):
    half = x.shape[0] // 2
    return jnp.where(low((half, 128)), x[:half], x[half:])


def expand(x):
    other = swap(x)
    side = low(x.shape)
    return jnp.concatenate([jnp.where(side, x, other), jnp.where(side, other, x)], axis=0)


def block_diagonal(x):
    side = low(x.shape)
    return jnp.concatenate([jnp.where(side, x, 0.0), jnp.where(side, 0.0, x)], axis=0)


def matmul(a, b):
    return jnp.dot(a, b, precision=HIGHEST, preferred_element_type=F32)


def gram_packed(x):
    full = matmul(x.T, x)
    own = jnp.where(low((RANK, 128)), full[:RANK] + swap(full[RANK:]), 0.0)
    return fold(own)


def scale_rows(gram, rows):
    r = lax.broadcasted_iota(jnp.int32, (RANK, 128), 0)
    c = lax.broadcasted_iota(jnp.int32, (RANK, 128), 1)
    both = jnp.where((c == r) | (c == r + RANK), gram, 0.0)
    across = jnp.sum(both, axis=0, keepdims=True)
    down = jnp.sum(jnp.where(c < RANK, both, 0.0), axis=1, keepdims=True)
    return jnp.sqrt(across / rows + 1e-06), jnp.sqrt(down / rows + 1e-06)


def inverse(system):
    lane = lax.broadcasted_iota(jnp.int32, (8, 128), 1) % RANK
    row = lax.broadcasted_iota(jnp.int32, (8, 128), 0)

    def row_of(x, n):
        return jnp.broadcast_to(x[n : n + 1], (8, 128))

    blocks = [system[8 * m : 8 * m + 8] for m in range(8)]
    for k in range(8):
        cols = [
            [jnp.broadcast_to(block[:, 8 * k + c : 8 * k + c + 1], (8, 128)) for c in range(8)]
            for block in blocks
        ]
        panel = (lane >= 8 * k) & (lane < 8 * k + 8)
        diag = list(cols[k])
        top = jnp.where(panel, jnp.where(lane == row + 8 * k, 1.0, 0.0), blocks[k])
        for c in range(8):
            pivot = 1.0 / row_of(diag[c], c)
            here = row == c
            factor = diag[c]
            line = row_of(top, c) * pivot
            top = jnp.where(here, line, top - factor * line)
            for d in range(c + 1, 8):
                line = row_of(diag[d], c) * pivot
                diag[d] = jnp.where(here, line, diag[d] - factor * line)
        lines = [row_of(top, c) for c in range(8)]
        for m in range(8):
            if m == k:
                blocks[m] = top
                continue
            less = [cols[m][c] * lines[c] for c in range(8)]
            while len(less) > 1:
                less = [less[n] + less[n + 1] for n in range(0, len(less), 2)]
            blocks[m] = jnp.where(panel, 0.0, blocks[m]) - less[0]
    return jnp.concatenate(blocks, axis=0)


def split(x):
    high = x.astype(BF16)
    return high, (x - high.astype(F32)).astype(BF16)


def kernel(
    t_ref, start_ref, out_ref,
    t32, thi, tlo, along, weights,
    c_one, c_all, b_one, b_all, b_packed,
    gb_slots, gc_slots, ma_part, ma_slots, ua_slots, ua_rows, a_columns,
    mb_part, mb_slots, mb_sum, ub, gu_slots, mc_part, mc_slot, mc_sum, ss_slots, rows_out,
    t_sem, send, recv, passed,
):
    gx, gy, gz = lax.axis_index("gx"), lax.axis_index("gy"), lax.axis_index("gz")
    z, x = gx // 4, lax.rem(gx, 4)
    yh, core = gz // 2, lax.rem(gz, 2)
    span_i = t_ref.shape[0]

    here = {"z": z, "x": x, "yh": yh, "gy": gy, "core": core}

    def group(*names):
        sizes = [SIZES[name] for name in names]

        def number(place):
            out = 0
            for name, size in zip(names, sizes):
                out = out * size + place[name]
            return out

        def hops(shift):
            shift = dict(zip(names, shift))
            y = 2 * shift.get("yh", 0) + shift.get("gy", 0)
            far = [min(n, 4 - n) for n in (shift.get("z", 0), shift.get("x", 0), y)]
            return sum(far) + 0.5 * shift.get("core", 0)

        shifts = sorted(itertools.product(*[range(size) for size in sizes]), key=hops, reverse=True)
        peers = []
        for shift in shifts[:-1]:
            place, source = dict(here), dict(here)
            for name, size, n in zip(names, sizes, shift):
                if n:
                    place[name] = lax.rem(here[name] + n, size)
                    source[name] = lax.rem(here[name] + size - n, size)
            device = (place["z"] * 4 + place["x"], place["gy"], place["yh"] * 2 + place["core"])
            peers.append((number(place), device, number(source)))
        return number(here), peers

    gy_me, gy_peers = group("gy")
    gz_me, gz_peers = group("yh", "core")
    gx_me, gx_peers = group("z", "x")
    _, x_peers = group("x")
    _, z_peers = group("z")
    yc_me, yc_peers = group("gy", "yh", "core")
    xc_me, xc_peers = group("x", "core")
    zh_me, zh_peers = group("z", "yh")

    pending = []
    used = [0]

    def start_one(peer, source, target):
        at = used[0]
        used[0] += 1
        copy = pltpu.make_async_remote_copy(
            src_ref=source,
            dst_ref=target,
            send_sem=send.at[at],
            recv_sem=recv.at[at],
            device_id=peer[1],
            device_id_type=MESH,
        )
        copy.start()
        pending.append(copy)
        return copy

    def start(peers, source, target):
        return [start_one(peer, source, target) for peer in peers]

    def arrive(copies):
        for copy in copies:
            copy.wait_recv()

    def add(total, copies, peers, slots):
        for copy, peer in zip(reversed(copies), reversed(peers)):
            copy.wait_recv()
            total = total + slots[peer[2]]
        return total

    def drain(keep=0):
        while len(pending) > keep:
            pending.pop(0).wait_send()

    barrier = pltpu.get_barrier_semaphore()
    greeted = z_peers + x_peers + yc_peers
    for peer in greeted:
        pl.semaphore_signal(barrier, inc=1, device_id=peer[1], device_id_type=MESH)
    c_one[gy] = start_ref[8:, :]
    b_one[gz] = start_ref[:8, :]

    def load(q):
        rows = pl.ds(q * GROUP, GROUP)
        return pltpu.make_async_copy(t_ref.at[rows], t32.at[rows], t_sem.at[q])

    def split_tensor(q, _):
        load(q).wait()

        def one(i, _):
            thi[i], tlo[i] = split(t32[i])
            return 0

        lax.fori_loop(q * GROUP, (q + 1) * GROUP, one, 0)
        return 0

    pl.semaphore_wait(barrier, len(greeted))

    for peer in z_peers:
        pl.semaphore_signal(passed, inc=1, device_id=peer[1], device_id_type=MESH)
    c_first = start(gy_peers, start_ref.at[pl.ds(8, 8)], c_one.at[gy])
    b_first = start(gz_peers, start_ref.at[pl.ds(0, 8)], b_one.at[gz])
    for q in range(span_i // GROUP):
        load(q).start()
    arrive(c_first)
    c_all[gx] = jnp.concatenate([c_one[0][:4], c_one[1][:4]], axis=1)
    pl.semaphore_wait(passed, len(z_peers))
    c_second = start(gx_peers, c_all.at[gx], c_all.at[gx])
    arrive(b_first)
    b_all[gx] = jnp.concatenate(
        [
            jnp.concatenate([b_one[0][:6], b_one[2][:6]], axis=1),
            jnp.concatenate([b_one[1][:6], b_one[3][:6]], axis=1),
        ],
        axis=0,
    )
    b_second = start(gx_peers, b_all.at[gx], b_all.at[gx])
    lax.fori_loop(0, span_i // GROUP, split_tensor, 0)
    drain(30)
    arrive(c_second)
    pieces = []
    for g in range(16):
        piece = c_all[g]
        other = swap(piece)
        side = low((4, 128))
        pieces += [jnp.where(side, piece, other), jnp.where(side, other, piece)]
    block_c = jnp.concatenate(pieces, axis=0)
    gram_c = matmul(block_c.T, block_c)[:RANK]
    gc_slots[gz] = compact(gram_c)
    gc_copies = start(gz_peers, gc_slots.at[gz], gc_slots.at[gz])
    c_high, c_low = split(block_c)
    side = low((128, 128))
    none = jnp.zeros((128, 128), BF16)
    weights[:128, :128] = jnp.where(side, c_high, none)
    weights[:128, 128:] = jnp.where(side, c_low, none)
    weights[128:, :128] = jnp.where(side, none, c_high)
    weights[128:, 128:] = jnp.where(side, none, c_low)

    half_j = along.shape[1]

    def wide(ref):
        return jnp.concatenate([ref[:, :half_j, :], ref[:, half_j:, :]], axis=2).reshape(span_i * half_j, 256)

    both = jnp.dot(wide(thi), weights[...], preferred_element_type=F32)
    rest = jnp.dot(wide(tlo), weights[:, :128], preferred_element_type=F32)
    along[...] = (both[:, :128] + (both[:, 128:] + rest)).reshape(along.shape)
    arrive(b_second)
    for g in range(8):
        one, two = b_all[g], b_all[g + 8]
        side = low((12, 128))
        b_packed[24 * g : 24 * g + 12, :] = jnp.where(side, one, swap(two))
        b_packed[24 * g + 12 : 24 * g + 24, :] = jnp.where(side, swap(one), two)
    block_b = b_packed[...]
    gb_slots[gy] = compact(gram_packed(block_b))
    gb_copies = start(gy_peers, gb_slots.at[gy], gb_slots.at[gy])
    def moment_a(i, _):
        product = along[i] * block_b
        ma_part[i] = jnp.sum(product.reshape(half_j // 8, 8, 128), axis=0)
        return 0

    lax.fori_loop(0, span_i, moment_a, 0)
    ma_slots[yc_me] = compact(fold(jnp.sum(ma_part[...], axis=1)))
    ma_copies = start(yc_peers, ma_slots.at[yc_me], ma_slots.at[yc_me])
    drain(7)
    arrive(gc_copies)
    arrive(gb_copies)
    gram_c = expand(gc_slots[0] + gc_slots[1] + gc_slots[2] + gc_slots[3])
    gram_b = expand(gb_slots[0] + gb_slots[1])
    inverse_a = block_diagonal(inverse(gram_b * gram_c))
    ua = matmul(add(ma_slots[yc_me], ma_copies, yc_peers, ma_slots), inverse_a)
    ua_slots[gx] = ua
    rows_a = expand(ua)
    for i in range(32):
        ua_rows[i] = jnp.broadcast_to(rows_a[i : i + 1], (8, 128))

    def moment_b(chunk):
        rows = pl.ds(pl.multiple_of(chunk * 24, 8), 24)
        total = jnp.zeros((3, 8, 128), F32)
        for q in range(4):
            some = along[8 * q : 8 * q + 8, rows, :].reshape(8, 3, 8, 128)
            total = total + jnp.sum(some * ua_rows[8 * q : 8 * q + 8][:, None], axis=0)
        return total.reshape(24, 128)

    mb_copies = []
    for peer in xc_peers:
        mb_part[peer[0]] = moment_b(peer[0])
        mb_copies.append(start_one(peer, mb_part.at[peer[0]], mb_slots.at[xc_me]))
    ua_copies = start(gx_peers, ua_slots.at[gx], ua_slots.at[gx])
    moment = moment_b(xc_me)
    drain(22)
    mb_sum[zh_me] = add(moment, mb_copies, xc_peers, mb_slots)
    mb_copies = start(zh_peers, mb_sum.at[zh_me], mb_sum.at[zh_me])
    arrive(ua_copies)
    gram_ua = gram_packed(ua_slots[...].reshape(256, 128))
    scale_a, scale_a_down = scale_rows(gram_ua, float(span_i * 16))
    gram_a = gram_ua / (scale_a * scale_a_down)
    inverse_b = block_diagonal(inverse(gram_a * gram_c))
    unscale_a = 1.0 / scale_a
    shard_a = ua_slots[gx] / scale_a
    full_a = expand(shard_a)
    turned = jnp.concatenate([full_a, full_a, full_a, full_a], axis=0).T
    for i in range(32):
        a_columns[i] = jnp.broadcast_to(turned[:RANK, i : i + 1], (RANK, 128))
    rows_out[:16, :] = jnp.where(gy == 0, shard_a, swap(shard_a))
    out_ref[:4, :] = rows_out[pl.ds(gz * 4, 4), :]
    drain(7)
    moment = add(mb_sum[zh_me], mb_copies, zh_peers, mb_sum)
    ub[xc_me] = matmul(moment * unscale_a, inverse_b)
    ub_copies = start(xc_peers, ub.at[xc_me], ub.at[xc_me])
    drain(7)
    arrive(ub_copies)

    block_b = ub[...].reshape(half_j, 128)
    turned = block_b.T
    turned_high, turned_low = split(turned)
    left = [
        jnp.concatenate([turned_high[h * RANK : (h + 1) * RANK], turned_low[h * RANK : (h + 1) * RANK]], axis=0)
        for h in range(2)
    ]
    left = jnp.concatenate(left, axis=1)

    moment = jnp.zeros((RANK, 128), F32)
    for i in range(0, span_i, 2):
        high = jnp.concatenate([thi[i], thi[i + 1]], axis=1)
        rest = jnp.concatenate([tlo[i], tlo[i + 1]], axis=1)
        part = jnp.dot(left, high, preferred_element_type=F32)
        part = part[:RANK] + (part[RANK:] + jnp.dot(left[:RANK], rest, preferred_element_type=F32))
        moment = moment + (part[:, :128] * a_columns[i] + part[:, 128:] * a_columns[i + 1])
    moment = compact(jnp.concatenate([moment, moment], axis=0).T)
    upper = lax.broadcasted_iota(jnp.int32, (8, 128), 0) < 4
    parts = [[], []]
    for m in range(4):
        one, two = moment[16 * m : 16 * m + 8], moment[16 * m + 8 : 16 * m + 16]
        parts[0].append(jnp.where(upper, one, pltpu.roll(two, 4, 0)))
        parts[1].append(jnp.where(upper, pltpu.roll(one, 4, 0), two))
    parts = [jnp.concatenate(part, axis=0) for part in parts]
    mc_part[...] = jnp.where(gy == 0, parts[1], parts[0])
    mc_copies = start(gy_peers, mc_part, mc_slot)
    gu_slots[gy] = compact(gram_packed(block_b))
    gu_copies = start(gy_peers, gu_slots.at[gy], gu_slots.at[gy])
    drain(2)
    arrive(mc_copies)
    mc_sum[gx] = jnp.where(gy == 0, parts[0], parts[1]) + mc_slot[...]
    mc_copies = start(gx_peers, mc_sum.at[gx], mc_sum.at[gx])
    arrive(gu_copies)
    gram_ub = expand(gu_slots[0] + gu_slots[1])
    scale_b, scale_b_down = scale_rows(gram_ub, float(half_j * 4))
    gram_b = gram_ub / (scale_b * scale_b_down)
    inverse_c = block_diagonal(inverse(gram_a * gram_b))
    unscale_b = 1.0 / scale_b
    shard_b = block_b / scale_b
    b_packed[...] = jnp.where(z // 2 == 0, shard_b, swap(shard_b))
    first = lax.rem(z, 2) * 96 + x * 24 + yh * 12 + core * 6
    out_ref[8:14, :] = b_packed[pl.ds(first, 6), :]
    drain(15)
    moment = add(mc_sum[gx], mc_copies, gx_peers, mc_sum)
    uc = matmul(moment * unscale_b, inverse_c)
    ss_slots[yc_me] = fold(jnp.sum(uc * uc, axis=0, keepdims=True))
    ss_copies = start(yc_peers, ss_slots.at[yc_me], ss_slots.at[yc_me])
    rows_out[...] = jnp.where(z // 2 == 0, uc, swap(uc))
    own = rows_out[pl.ds(lax.rem(gx, 8) * 4, 4), :]
    drain(7)
    total = add(ss_slots[yc_me], ss_copies, yc_peers, ss_slots)
    out_ref[4:8, :] = own / jnp.sqrt(total / float(128 * 4) + 1e-06)
    drain()


COPIES = 1 + 3 + 15 + 15 + 3 + 1 + 7 + 7 + 15 + 7 + 7 + 1 + 1 + 15 + 7


def local(tensor, factor_b, factor_c):
    span_i, span_j, span_k = tensor.shape
    half_j = span_j // 2
    vmem = pl.BlockSpec(memory_space=pltpu.VMEM)
    scratch = [
        pltpu.VMEM(tensor.shape, F32),
        pltpu.VMEM(tensor.shape, BF16),
        pltpu.VMEM(tensor.shape, BF16),
        pltpu.VMEM((span_i, half_j, 128), F32),
        pltpu.VMEM((256, 256), BF16),
        pltpu.VMEM((2, 8, RANK), F32),
        pltpu.VMEM((16, 4, 128), F32),
        pltpu.VMEM((4, 8, RANK), F32),
        pltpu.VMEM((16, 12, 128), F32),
        pltpu.VMEM((half_j, 128), F32),
        pltpu.VMEM((2, 32, 128), F32),
        pltpu.VMEM((4, 32, 128), F32),
        pltpu.VMEM((span_i, 8, 128), F32),
        pltpu.VMEM((8, 16, 128), F32),
        pltpu.VMEM((16, 16, 128), F32),
        pltpu.VMEM((32, 8, 128), F32),
        pltpu.VMEM((32, RANK, 128), F32),
        pltpu.VMEM((8, 24, 128), F32),
        pltpu.VMEM((8, 24, 128), F32),
        pltpu.VMEM((8, 24, 128), F32),
        pltpu.VMEM((8, 24, 128), F32),
        pltpu.VMEM((2, 32, 128), F32),
        pltpu.VMEM((32, 128), F32),
        pltpu.VMEM((32, 128), F32),
        pltpu.VMEM((16, 32, 128), F32),
        pltpu.VMEM((8, 1, 128), F32),
        pltpu.VMEM((32, 128), F32),
        pltpu.SemaphoreType.DMA((span_i // GROUP,)),
        pltpu.SemaphoreType.DMA((COPIES,)),
        pltpu.SemaphoreType.DMA((COPIES,)),
        pltpu.SemaphoreType.REGULAR,
    ]
    start = jnp.concatenate(
        [jnp.pad(factor_b, ((0, 2), (0, 0))), jnp.pad(factor_c, ((0, 4), (0, 0)))], axis=0
    )
    out = pl.pallas_call(
        kernel,
        out_shape=jax.ShapeDtypeStruct((16, 128), F32),
        in_specs=[pl.BlockSpec(memory_space=pl.ANY), vmem],
        out_specs=vmem,
        scratch_shapes=scratch,
        compiler_params=pltpu.CompilerParams(
            collective_id=0, has_side_effects=True, vmem_limit_bytes=48 * 1024 * 1024
        ),
    )(tensor, start)
    return out[:4, :RANK], out[8:14, :RANK], out[4:8, :RANK]


def solution(mesh):
    return jax.shard_map(
        local,
        mesh=mesh,
        in_specs=(P("gx", "gy", "gz"), P(("gy", "gx", "gz"), None), P(("gz", "gx", "gy"), None)),
        out_specs=(
            P(("gx", "gy", "gz"), None),
            P(("gy", "gx", "gz"), None),
            P(("gz", "gx", "gy"), None),
        ),
        check_vma=False,
    )
```

```python
import itertools

import jax
import jax.numpy as jnp
from jax import lax
from jax.experimental import pallas as pl
from jax.experimental.pallas import tpu as pltpu
from jax.sharding import PartitionSpec as P

MESH = pl.DeviceIdType.MESH
HIGHEST = lax.Precision.HIGHEST
F32 = jnp.float32
BF16 = jnp.bfloat16

RANK = 64
GROUP = 8
SIZES = {"z": 4, "x": 4, "yh": 2, "gy": 2, "core": 2}


def low(shape):
    return lax.broadcasted_iota(jnp.int32, shape, 1) < RANK


def swap(x):
    return pltpu.roll(x, RANK, 1)


def fold(x):
    return x + swap(x)


def compact(x):
    half = x.shape[0] // 2
    return jnp.where(low((half, 128)), x[:half], x[half:])


def expand(x):
    other = swap(x)
    side = low(x.shape)
    return jnp.concatenate([jnp.where(side, x, other), jnp.where(side, other, x)], axis=0)


def block_diagonal(x):
    side = low(x.shape)
    return jnp.concatenate([jnp.where(side, x, 0.0), jnp.where(side, 0.0, x)], axis=0)


def matmul(a, b):
    return jnp.dot(a, b, precision=HIGHEST, preferred_element_type=F32)


def gram_packed(x):
    full = matmul(x.T, x)
    own = jnp.where(low((RANK, 128)), full[:RANK] + swap(full[RANK:]), 0.0)
    return fold(own)


def scale_rows(gram, rows):
    r = lax.broadcasted_iota(jnp.int32, (RANK, 128), 0)
    c = lax.broadcasted_iota(jnp.int32, (RANK, 128), 1)
    both = jnp.where((c == r) | (c == r + RANK), gram, 0.0)
    across = jnp.sum(both, axis=0, keepdims=True)
    down = jnp.sum(jnp.where(c < RANK, both, 0.0), axis=1, keepdims=True)
    return jnp.sqrt(across / rows + 1e-06), jnp.sqrt(down / rows + 1e-06)


def inverse(system):
    lane = lax.broadcasted_iota(jnp.int32, (8, 128), 1) % RANK
    row = lax.broadcasted_iota(jnp.int32, (8, 128), 0)

    def row_of(x, n):
        return jnp.broadcast_to(x[n : n + 1], (8, 128))

    blocks = [system[8 * m : 8 * m + 8] for m in range(8)]
    for k in range(8):
        cols = [
            [jnp.broadcast_to(block[:, 8 * k + c : 8 * k + c + 1], (8, 128)) for c in range(8)]
            for block in blocks
        ]
        panel = (lane >= 8 * k) & (lane < 8 * k + 8)
        diag = list(cols[k])
        top = jnp.where(panel, jnp.where(lane == row + 8 * k, 1.0, 0.0), blocks[k])
        for c in range(8):
            pivot = 1.0 / row_of(diag[c], c)
            here = row == c
            factor = diag[c]
            line = row_of(top, c) * pivot
            top = jnp.where(here, line, top - factor * line)
            for d in range(c + 1, 8):
                line = row_of(diag[d], c) * pivot
                diag[d] = jnp.where(here, line, diag[d] - factor * line)
        lines = [row_of(top, c) for c in range(8)]
        for m in range(8):
            if m == k:
                blocks[m] = top
                continue
            less = [cols[m][c] * lines[c] for c in range(8)]
            while len(less) > 1:
                less = [less[n] + less[n + 1] for n in range(0, len(less), 2)]
            blocks[m] = jnp.where(panel, 0.0, blocks[m]) - less[0]
    return jnp.concatenate(blocks, axis=0)


def split(x):
    high = x.astype(BF16)
    return high, (x - high.astype(F32)).astype(BF16)


def kernel(
    t_ref, start_ref, out_ref,
    t32, thi, tlo, along, weights,
    c_one, c_all, b_one, b_all, b_packed,
    gb_slots, gc_slots, ma_part, ma_slots, ua_slots, ua_rows, a_columns,
    mb_part, mb_slots, mb_sum, ub, gu_slots, mc_part, mc_slot, mc_sum, ss_slots, rows_out,
    t_sem, send, recv, passed,
):
    gx, gy, gz = lax.axis_index("gx"), lax.axis_index("gy"), lax.axis_index("gz")
    z, x = gx // 4, lax.rem(gx, 4)
    yh, core = gz // 2, lax.rem(gz, 2)
    span_i = t_ref.shape[0]

    here = {"z": z, "x": x, "yh": yh, "gy": gy, "core": core}

    def group(*names):
        sizes = [SIZES[name] for name in names]

        def number(place):
            out = 0
            for name, size in zip(names, sizes):
                out = out * size + place[name]
            return out

        def hops(shift):
            shift = dict(zip(names, shift))
            y = 2 * shift.get("yh", 0) + shift.get("gy", 0)
            far = [min(n, 4 - n) for n in (shift.get("z", 0), shift.get("x", 0), y)]
            return sum(far) + 0.5 * shift.get("core", 0)

        shifts = sorted(itertools.product(*[range(size) for size in sizes]), key=hops, reverse=True)
        peers = []
        for shift in shifts[:-1]:
            place, source = dict(here), dict(here)
            for name, size, n in zip(names, sizes, shift):
                if n:
                    place[name] = lax.rem(here[name] + n, size)
                    source[name] = lax.rem(here[name] + size - n, size)
            device = (place["z"] * 4 + place["x"], place["gy"], place["yh"] * 2 + place["core"])
            peers.append((number(place), device, number(source)))
        return number(here), peers, shifts[:-1]

    gy_me, gy_peers, _ = group("gy")
    gz_me, gz_peers, _ = group("yh", "core")
    gx_me, gx_peers, _ = group("z", "x")
    _, x_peers, _ = group("x")
    _, z_peers, _ = group("z")
    yc_me, yc_peers, _ = group("gy", "yh", "core")
    xc_me, xc_peers, xc_shifts = group("x", "core")
    zh_me, zh_peers, _ = group("z", "yh")

    pending = []
    used = [0]

    def start_one(peer, source, target):
        at = used[0]
        used[0] += 1
        copy = pltpu.make_async_remote_copy(
            src_ref=source,
            dst_ref=target,
            send_sem=send.at[at],
            recv_sem=recv.at[at],
            device_id=peer[1],
            device_id_type=MESH,
        )
        copy.start()
        pending.append(copy)
        return copy

    def start(peers, source, target):
        return [start_one(peer, source, target) for peer in peers]

    def arrive(copies):
        for copy in copies:
            copy.wait_recv()

    def add(total, copies, peers, slots):
        for copy, peer in zip(reversed(copies), reversed(peers)):
            copy.wait_recv()
            total = total + slots[peer[2]]
        return total

    def drain(keep=0):
        while len(pending) > keep:
            pending.pop(0).wait_send()

    barrier = pltpu.get_barrier_semaphore()
    greeted = z_peers + x_peers + yc_peers
    for peer in greeted:
        pl.semaphore_signal(barrier, inc=1, device_id=peer[1], device_id_type=MESH)
    c_one[gy] = start_ref[8:, :]
    b_one[gz] = start_ref[:8, :]

    def load(q):
        rows = pl.ds(q * GROUP, GROUP)
        return pltpu.make_async_copy(t_ref.at[rows], t32.at[rows], t_sem.at[q])

    def split_tensor(q, _):
        load(q).wait()

        def one(i, _):
            thi[i], tlo[i] = split(t32[i])
            return 0

        lax.fori_loop(q * GROUP, (q + 1) * GROUP, one, 0)
        return 0

    pl.semaphore_wait(barrier, len(greeted))

    for peer in z_peers:
        pl.semaphore_signal(passed, inc=1, device_id=peer[1], device_id_type=MESH)
    c_first = start(gy_peers, start_ref.at[pl.ds(8, 8)], c_one.at[gy])
    b_first = start(gz_peers, start_ref.at[pl.ds(0, 8)], b_one.at[gz])
    for q in range(span_i // GROUP):
        load(q).start()
    arrive(c_first)
    rows_c = jnp.concatenate([c_one[0][:4], c_one[1][:4]], axis=0)
    c_all[gx] = jnp.concatenate([rows_c, rows_c], axis=1)
    pl.semaphore_wait(passed, len(z_peers))
    c_second = start(gx_peers, c_all.at[gx], c_all.at[gx])
    arrive(b_first)
    b_all[gx] = jnp.concatenate(
        [
            jnp.concatenate([b_one[0][:6], b_one[2][:6]], axis=1),
            jnp.concatenate([b_one[1][:6], b_one[3][:6]], axis=1),
        ],
        axis=0,
    )
    b_second = start(gx_peers, b_all.at[gx], b_all.at[gx])
    lax.fori_loop(0, span_i // GROUP, split_tensor, 0)
    drain(30)
    arrive(c_second)
    block_c = c_all[...].reshape(128, 128)
    gram_c = matmul(block_c.T, block_c)[:RANK]
    gc_slots[gz] = compact(gram_c)
    gc_copies = start(gz_peers, gc_slots.at[gz], gc_slots.at[gz])
    c_high, c_low = split(block_c)
    side = low((128, 128))
    none = jnp.zeros((128, 128), BF16)
    weights[:128, :128] = jnp.where(side, c_high, none)
    weights[:128, 128:] = jnp.where(side, c_low, none)
    weights[128:, :128] = jnp.where(side, none, c_high)
    weights[128:, 128:] = jnp.where(side, none, c_low)

    half_j = along.shape[1]

    arrive(b_second)
    for g in range(8):
        one, two = b_all[g], b_all[g + 8]
        side = low((12, 128))
        b_packed[24 * g : 24 * g + 12, :] = jnp.where(side, one, swap(two))
        b_packed[24 * g + 12 : 24 * g + 24, :] = jnp.where(side, swap(one), two)
    block_b = b_packed[...]
    gb_slots[gy] = compact(gram_packed(block_b))
    gb_copies = start(gy_peers, gb_slots.at[gy], gb_slots.at[gy])
    for q in range(0, span_i, 2):

        def wide(ref):
            left, right = ref[q : q + 2, :half_j, :], ref[q : q + 2, half_j:, :]
            return jnp.concatenate([left, right], axis=2).reshape(2 * half_j, 256)

        both = jnp.dot(wide(thi), weights[...], preferred_element_type=F32)
        rest = jnp.dot(wide(tlo), weights[:, :128], preferred_element_type=F32)
        pair = (both[:, :128] + (both[:, 128:] + rest)).reshape(2, half_j, 128)
        along[q : q + 2] = pair
        for n in range(2):
            ma_part[q + n] = jnp.sum((pair[n] * block_b).reshape(half_j // 8, 8, 128), axis=0)
    ma_slots[yc_me] = compact(fold(jnp.sum(ma_part[...], axis=1)))
    ma_copies = start(yc_peers, ma_slots.at[yc_me], ma_slots.at[yc_me])
    drain(7)
    arrive(gc_copies)
    arrive(gb_copies)
    gram_c = expand(gc_slots[0] + gc_slots[1] + gc_slots[2] + gc_slots[3])
    gram_b = expand(gb_slots[0] + gb_slots[1])
    inverse_a = block_diagonal(inverse(gram_b * gram_c))
    ua = matmul(add(ma_slots[yc_me], ma_copies, yc_peers, ma_slots), inverse_a)
    ua_slots[gx] = ua
    rows_a = expand(ua)
    for i in range(32):
        ua_rows[i] = jnp.broadcast_to(rows_a[i : i + 1], (8, 128))

    def moment_b(chunk):
        rows = pl.ds(pl.multiple_of(chunk * 24, 8), 24)
        total = jnp.zeros((3, 8, 128), F32)
        for q in range(4):
            some = along[8 * q : 8 * q + 8, rows, :].reshape(8, 3, 8, 128)
            total = total + jnp.sum(some * ua_rows[8 * q : 8 * q + 8][:, None], axis=0)
        return total.reshape(24, 128)

    mb_copies = []
    for peer in xc_peers:
        mb_part[peer[0]] = moment_b(peer[0])
        mb_copies.append(start_one(peer, mb_part.at[peer[0]], mb_slots.at[xc_me]))
    ua_copies = start(gx_peers, ua_slots.at[gx], ua_slots.at[gx])
    moment = moment_b(xc_me)
    drain(22)
    mb_sum[zh_me] = add(moment, mb_copies, xc_peers, mb_slots)
    mb_copies = start(zh_peers, mb_sum.at[zh_me], mb_sum.at[zh_me])
    arrive(ua_copies)
    gram_ua = gram_packed(ua_slots[...].reshape(256, 128))
    scale_a, scale_a_down = scale_rows(gram_ua, float(span_i * 16))
    gram_a = gram_ua / (scale_a * scale_a_down)
    inverse_b = block_diagonal(inverse(gram_a * gram_c))
    unscale_a = 1.0 / scale_a
    moment = add(mb_sum[zh_me], mb_copies, zh_peers, mb_sum)
    ub[xc_me] = matmul(moment * unscale_a, inverse_b)
    ub_copies = start(xc_peers, ub.at[xc_me], ub.at[xc_me])
    shard_a = ua_slots[gx] / scale_a
    full_a = expand(shard_a)
    turned = jnp.concatenate([full_a, full_a, full_a, full_a], axis=0).T
    for i in range(32):
        a_columns[i] = jnp.broadcast_to(turned[:RANK, i : i + 1], (RANK, 128))
    rows_out[:16, :] = jnp.where(gy == 0, shard_a, swap(shard_a))
    out_ref[:4, :] = rows_out[pl.ds(gz * 4, 4), :]
    drain(7)
    arrivals = list(zip(ub_copies, xc_peers, xc_shifts))
    moment = jnp.zeros((RANK, 128), F32)
    for near in (True, False):
        for copy, peer, shift in reversed(arrivals):
            if (shift[0] in (0, 1)) == near:
                copy.wait_recv()
        ends = [x, lax.rem(x + 3, 4)] if near else [lax.rem(x + 1, 4), lax.rem(x + 2, 4)]
        own = [ub[pl.ds(2 * end, 2)].reshape(48, 128) for end in ends]
        turned_high, turned_low = split(jnp.concatenate(own, axis=0).T)
        left = jnp.concatenate(
            [
                jnp.concatenate([turned_high[:RANK], turned_high[RANK:]], axis=1),
                jnp.concatenate([turned_low[:RANK], turned_low[RANK:]], axis=1),
            ],
            axis=0,
        )

        def rows_of(ref, i):
            return jnp.concatenate(
                [
                    ref[i, pl.ds(pl.multiple_of(h * half_j + end * 48, 16), 48), :]
                    for h in range(2)
                    for end in ends
                ],
                axis=0,
            )

        for i in range(0, span_i, 2):
            high = jnp.concatenate([rows_of(thi, i), rows_of(thi, i + 1)], axis=1)
            rest = jnp.concatenate([rows_of(tlo, i), rows_of(tlo, i + 1)], axis=1)
            part = jnp.dot(left, high, preferred_element_type=F32)
            part = part[:RANK] + (part[RANK:] + jnp.dot(left[:RANK], rest, preferred_element_type=F32))
            moment = moment + (part[:, :128] * a_columns[i] + part[:, 128:] * a_columns[i + 1])
    block_b = ub[...].reshape(half_j, 128)
    moment = compact(jnp.concatenate([moment, moment], axis=0).T)
    upper = lax.broadcasted_iota(jnp.int32, (8, 128), 0) < 4
    parts = [[], []]
    for m in range(4):
        one, two = moment[16 * m : 16 * m + 8], moment[16 * m + 8 : 16 * m + 16]
        parts[0].append(jnp.where(upper, one, pltpu.roll(two, 4, 0)))
        parts[1].append(jnp.where(upper, pltpu.roll(one, 4, 0), two))
    parts = [jnp.concatenate(part, axis=0) for part in parts]
    mc_part[...] = jnp.where(gy == 0, parts[1], parts[0])
    mc_copies = start(gy_peers, mc_part, mc_slot)
    gu_slots[gy] = compact(gram_packed(block_b))
    gu_copies = start(gy_peers, gu_slots.at[gy], gu_slots.at[gy])
    drain(2)
    arrive(mc_copies)
    mc_sum[gx] = jnp.where(gy == 0, parts[0], parts[1]) + mc_slot[...]
    mc_copies = start(gx_peers, mc_sum.at[gx], mc_sum.at[gx])
    arrive(gu_copies)
    gram_ub = expand(gu_slots[0] + gu_slots[1])
    scale_b, scale_b_down = scale_rows(gram_ub, float(half_j * 4))
    gram_b = gram_ub / (scale_b * scale_b_down)
    inverse_c = block_diagonal(inverse(gram_a * gram_b))
    unscale_b = 1.0 / scale_b
    shard_b = block_b / scale_b
    b_packed[...] = jnp.where(z // 2 == 0, shard_b, swap(shard_b))
    first = lax.rem(z, 2) * 96 + x * 24 + yh * 12 + core * 6
    out_ref[8:14, :] = b_packed[pl.ds(first, 6), :]
    drain(15)
    moment = add(mc_sum[gx], mc_copies, gx_peers, mc_sum)
    uc = matmul(moment * unscale_b, inverse_c)
    ss_slots[yc_me] = fold(jnp.sum(uc * uc, axis=0, keepdims=True))
    ss_copies = start(yc_peers, ss_slots.at[yc_me], ss_slots.at[yc_me])
    rows_out[...] = jnp.where(z // 2 == 0, uc, swap(uc))
    own = rows_out[pl.ds(lax.rem(gx, 8) * 4, 4), :]
    drain(7)
    total = add(ss_slots[yc_me], ss_copies, yc_peers, ss_slots)
    out_ref[4:8, :] = own / jnp.sqrt(total / float(128 * 4) + 1e-06)
    drain()


COPIES = 1 + 3 + 15 + 15 + 3 + 1 + 7 + 7 + 15 + 7 + 7 + 1 + 1 + 15 + 7


def local(tensor, factor_b, factor_c):
    span_i, span_j, span_k = tensor.shape
    half_j = span_j // 2
    vmem = pl.BlockSpec(memory_space=pltpu.VMEM)
    scratch = [
        pltpu.VMEM(tensor.shape, F32),
        pltpu.VMEM(tensor.shape, BF16),
        pltpu.VMEM(tensor.shape, BF16),
        pltpu.VMEM((span_i, half_j, 128), F32),
        pltpu.VMEM((256, 256), BF16),
        pltpu.VMEM((2, 8, RANK), F32),
        pltpu.VMEM((16, 8, 128), F32),
        pltpu.VMEM((4, 8, RANK), F32),
        pltpu.VMEM((16, 12, 128), F32),
        pltpu.VMEM((half_j, 128), F32),
        pltpu.VMEM((2, 32, 128), F32),
        pltpu.VMEM((4, 32, 128), F32),
        pltpu.VMEM((span_i, 8, 128), F32),
        pltpu.VMEM((8, 16, 128), F32),
        pltpu.VMEM((16, 16, 128), F32),
        pltpu.VMEM((32, 8, 128), F32),
        pltpu.VMEM((32, RANK, 128), F32),
        pltpu.VMEM((8, 24, 128), F32),
        pltpu.VMEM((8, 24, 128), F32),
        pltpu.VMEM((8, 24, 128), F32),
        pltpu.VMEM((8, 24, 128), F32),
        pltpu.VMEM((2, 32, 128), F32),
        pltpu.VMEM((32, 128), F32),
        pltpu.VMEM((32, 128), F32),
        pltpu.VMEM((16, 32, 128), F32),
        pltpu.VMEM((8, 1, 128), F32),
        pltpu.VMEM((32, 128), F32),
        pltpu.SemaphoreType.DMA((span_i // GROUP,)),
        pltpu.SemaphoreType.DMA((COPIES,)),
        pltpu.SemaphoreType.DMA((COPIES,)),
        pltpu.SemaphoreType.REGULAR,
    ]
    start = jnp.concatenate(
        [jnp.pad(factor_b, ((0, 2), (0, 0))), jnp.pad(factor_c, ((0, 4), (0, 0)))], axis=0
    )
    out = pl.pallas_call(
        kernel,
        out_shape=jax.ShapeDtypeStruct((16, 128), F32),
        in_specs=[pl.BlockSpec(memory_space=pl.ANY), vmem],
        out_specs=vmem,
        scratch_shapes=scratch,
        compiler_params=pltpu.CompilerParams(
            collective_id=0, has_side_effects=True, vmem_limit_bytes=48 * 1024 * 1024
        ),
    )(tensor, start)
    return out[:4, :RANK], out[8:14, :RANK], out[4:8, :RANK]


def solution(mesh):
    return jax.shard_map(
        local,
        mesh=mesh,
        in_specs=(P("gx", "gy", "gz"), P(("gy", "gx", "gz"), None), P(("gz", "gx", "gy"), None)),
        out_specs=(
            P(("gx", "gy", "gz"), None),
            P(("gy", "gx", "gz"), None),
            P(("gz", "gx", "gy"), None),
        ),
        check_vma=False,
    )
```

```python
import itertools

import jax
import jax.numpy as jnp
from jax import lax
from jax.experimental import pallas as pl
from jax.experimental.pallas import tpu as pltpu
from jax.sharding import PartitionSpec as P

MESH = pl.DeviceIdType.MESH
HIGHEST = lax.Precision.HIGHEST
F32 = jnp.float32
BF16 = jnp.bfloat16

RANK = 64
GROUP = 8
SIZES = {"z": 4, "x": 4, "yh": 2, "gy": 2, "core": 2}


def low(shape):
    return lax.broadcasted_iota(jnp.int32, shape, 1) < RANK


def swap(x):
    return pltpu.roll(x, RANK, 1)


def fold(x):
    return x + swap(x)


def compact(x):
    half = x.shape[0] // 2
    return jnp.where(low((half, 128)), x[:half], x[half:])


def expand(x):
    other = swap(x)
    side = low(x.shape)
    return jnp.concatenate([jnp.where(side, x, other), jnp.where(side, other, x)], axis=0)


def block_diagonal(x):
    side = low(x.shape)
    return jnp.concatenate([jnp.where(side, x, 0.0), jnp.where(side, 0.0, x)], axis=0)


def matmul(a, b):
    return jnp.dot(a, b, precision=HIGHEST, preferred_element_type=F32)


def gram_packed(x):
    full = matmul(x.T, x)
    own = jnp.where(low((RANK, 128)), full[:RANK] + swap(full[RANK:]), 0.0)
    return fold(own)


def scale_rows(gram, rows):
    r = lax.broadcasted_iota(jnp.int32, (RANK, 128), 0)
    c = lax.broadcasted_iota(jnp.int32, (RANK, 128), 1)
    both = jnp.where((c == r) | (c == r + RANK), gram, 0.0)
    across = jnp.sum(both, axis=0, keepdims=True)
    down = jnp.sum(jnp.where(c < RANK, both, 0.0), axis=1, keepdims=True)
    return jnp.sqrt(across / rows + 1e-06), jnp.sqrt(down / rows + 1e-06)


def inverse(system):
    lane = lax.broadcasted_iota(jnp.int32, (8, 128), 1) % RANK
    row = lax.broadcasted_iota(jnp.int32, (8, 128), 0)

    def row_of(x, n):
        return jnp.broadcast_to(x[n : n + 1], (8, 128))

    blocks = [system[8 * m : 8 * m + 8] for m in range(8)]
    for k in range(8):
        cols = [
            [jnp.broadcast_to(block[:, 8 * k + c : 8 * k + c + 1], (8, 128)) for c in range(8)]
            for block in blocks
        ]
        panel = (lane >= 8 * k) & (lane < 8 * k + 8)
        diag = list(cols[k])
        top = jnp.where(panel, jnp.where(lane == row + 8 * k, 1.0, 0.0), blocks[k])
        for c in range(8):
            pivot = 1.0 / row_of(diag[c], c)
            here = row == c
            factor = diag[c]
            line = row_of(top, c) * pivot
            top = jnp.where(here, line, top - factor * line)
            for d in range(c + 1, 8):
                line = row_of(diag[d], c) * pivot
                diag[d] = jnp.where(here, line, diag[d] - factor * line)
        lines = [row_of(top, c) for c in range(8)]
        for m in range(8):
            if m == k:
                blocks[m] = top
                continue
            less = [cols[m][c] * lines[c] for c in range(8)]
            while len(less) > 1:
                less = [less[n] + less[n + 1] for n in range(0, len(less), 2)]
            blocks[m] = jnp.where(panel, 0.0, blocks[m]) - less[0]
    return jnp.concatenate(blocks, axis=0)


def split(x):
    high = x.astype(BF16)
    return high, (x - high.astype(F32)).astype(BF16)


def kernel(
    t_ref, start_ref, out_ref,
    t32, thi, tlo, along, weights,
    c_one, c_all, b_one, b_all, b_packed,
    gb_slots, gc_slots, ma_part, ma_slots, ua_slots, ua_rows, a_columns,
    mb_part, mb_slots, mb_sum, ub, gu_slots, mc_part, mc_slot, mc_sum, ss_slots, rows_out,
    t_sem, send, recv, passed,
):
    gx, gy, gz = lax.axis_index("gx"), lax.axis_index("gy"), lax.axis_index("gz")
    z, x = gx // 4, lax.rem(gx, 4)
    yh, core = gz // 2, lax.rem(gz, 2)
    span_i = t_ref.shape[0]

    here = {"z": z, "x": x, "yh": yh, "gy": gy, "core": core}

    def group(*names):
        sizes = [SIZES[name] for name in names]

        def number(place):
            out = 0
            for name, size in zip(names, sizes):
                out = out * size + place[name]
            return out

        def hops(shift):
            shift = dict(zip(names, shift))
            y = 2 * shift.get("yh", 0) + shift.get("gy", 0)
            far = [min(n, 4 - n) for n in (shift.get("z", 0), shift.get("x", 0), y)]
            return sum(far) + 0.5 * shift.get("core", 0)

        shifts = sorted(itertools.product(*[range(size) for size in sizes]), key=hops, reverse=True)
        peers = []
        for shift in shifts[:-1]:
            place, source = dict(here), dict(here)
            for name, size, n in zip(names, sizes, shift):
                if n:
                    place[name] = lax.rem(here[name] + n, size)
                    source[name] = lax.rem(here[name] + size - n, size)
            device = (place["z"] * 4 + place["x"], place["gy"], place["yh"] * 2 + place["core"])
            peers.append((number(place), device, number(source)))
        return number(here), peers, shifts[:-1]

    gy_me, gy_peers, _ = group("gy")
    gz_me, gz_peers, _ = group("yh", "core")
    gx_me, gx_peers, _ = group("z", "x")
    _, x_peers, _ = group("x")
    _, z_peers, _ = group("z")
    yc_me, yc_peers, _ = group("gy", "yh", "core")
    xc_me, xc_peers, xc_shifts = group("x", "core")
    zh_me, zh_peers, _ = group("z", "yh")

    pending = []
    used = [0]

    def start_one(peer, source, target):
        at = used[0]
        used[0] += 1
        copy = pltpu.make_async_remote_copy(
            src_ref=source,
            dst_ref=target,
            send_sem=send.at[at],
            recv_sem=recv.at[at],
            device_id=peer[1],
            device_id_type=MESH,
        )
        copy.start()
        pending.append(copy)
        return copy

    def start(peers, source, target):
        return [start_one(peer, source, target) for peer in peers]

    def arrive(copies):
        for copy in copies:
            copy.wait_recv()

    def add(total, copies, peers, slots):
        for copy, peer in zip(reversed(copies), reversed(peers)):
            copy.wait_recv()
            total = total + slots[peer[2]]
        return total

    def drain(keep=0):
        while len(pending) > keep:
            pending.pop(0).wait_send()

    barrier = pltpu.get_barrier_semaphore()
    greeted = z_peers + x_peers + yc_peers
    for peer in greeted:
        pl.semaphore_signal(barrier, inc=1, device_id=peer[1], device_id_type=MESH)
    c_one[gy] = start_ref[8:, :]
    b_one[gz] = start_ref[:8, :]

    def load(q):
        rows = pl.ds(q * GROUP, GROUP)
        return pltpu.make_async_copy(t_ref.at[rows], t32.at[rows], t_sem.at[q])

    def split_tensor(q, _):
        load(q).wait()

        def one(i, _):
            thi[i], tlo[i] = split(t32[i])
            return 0

        lax.fori_loop(q * GROUP, (q + 1) * GROUP, one, 0)
        return 0

    pl.semaphore_wait(barrier, len(greeted))

    for peer in z_peers:
        pl.semaphore_signal(passed, inc=1, device_id=peer[1], device_id_type=MESH)
    c_first = start(gy_peers, start_ref.at[pl.ds(8, 8)], c_one.at[gy])
    b_first = start(gz_peers, start_ref.at[pl.ds(0, 8)], b_one.at[gz])
    for q in range(span_i // GROUP):
        load(q).start()
    arrive(c_first)
    rows_c = jnp.concatenate([c_one[0][:4], c_one[1][:4]], axis=0)
    c_all[gx] = jnp.concatenate([rows_c, rows_c], axis=1)
    pl.semaphore_wait(passed, len(z_peers))
    c_second = start(gx_peers, c_all.at[gx], c_all.at[gx])
    arrive(b_first)
    b_all[gx] = jnp.concatenate(
        [
            jnp.concatenate([b_one[0][:6], b_one[2][:6]], axis=1),
            jnp.concatenate([b_one[1][:6], b_one[3][:6]], axis=1),
        ],
        axis=0,
    )
    b_second = start(gx_peers, b_all.at[gx], b_all.at[gx])
    lax.fori_loop(0, span_i // GROUP, split_tensor, 0)
    drain(30)
    arrive(c_second)
    block_c = c_all[...].reshape(128, 128)
    gram_c = matmul(block_c.T, block_c)[:RANK]
    gc_slots[gz] = compact(gram_c)
    gc_copies = start(gz_peers, gc_slots.at[gz], gc_slots.at[gz])
    c_high, c_low = split(block_c)
    side = low((128, 128))
    none = jnp.zeros((128, 128), BF16)
    weights[:128, :128] = jnp.where(side, c_high, none)
    weights[:128, 128:] = jnp.where(side, c_low, none)
    weights[128:, :128] = jnp.where(side, none, c_high)
    weights[128:, 128:] = jnp.where(side, none, c_low)

    half_j = along.shape[1]

    arrive(b_second)
    for g in range(8):
        one, two = b_all[g], b_all[g + 8]
        side = low((12, 128))
        b_packed[24 * g : 24 * g + 12, :] = jnp.where(side, one, swap(two))
        b_packed[24 * g + 12 : 24 * g + 24, :] = jnp.where(side, swap(one), two)
    block_b = b_packed[:half_j, :]
    gb_slots[gy] = compact(gram_packed(block_b))
    gb_copies = start(gy_peers, gb_slots.at[gy], gb_slots.at[gy])
    for q in range(0, span_i, 2):

        def wide(ref):
            left, right = ref[q : q + 2, :half_j, :], ref[q : q + 2, half_j:, :]
            return jnp.concatenate([left, right], axis=2).reshape(2 * half_j, 256)

        both = jnp.dot(wide(thi), weights[...], preferred_element_type=F32)
        rest = jnp.dot(wide(tlo), weights[:, :128], preferred_element_type=F32)
        pair = (both[:, :128] + (both[:, 128:] + rest)).reshape(2, half_j, 128)
        along[q : q + 2] = pair
        for n in range(2):
            ma_part[q + n] = jnp.sum((pair[n] * block_b).reshape(half_j // 8, 8, 128), axis=0)
    ma_slots[yc_me] = compact(fold(jnp.sum(ma_part[...], axis=1)))
    ma_copies = start(yc_peers, ma_slots.at[yc_me], ma_slots.at[yc_me])
    drain(7)
    arrive(gc_copies)
    arrive(gb_copies)
    gram_c = expand(gc_slots[0] + gc_slots[1] + gc_slots[2] + gc_slots[3])
    gram_b = expand(gb_slots[0] + gb_slots[1])
    inverse_a = block_diagonal(inverse(gram_b * gram_c))
    ua = matmul(add(ma_slots[yc_me], ma_copies, yc_peers, ma_slots), inverse_a)
    ua_slots[gx] = ua
    rows_a = expand(ua)
    for i in range(32):
        ua_rows[i] = jnp.broadcast_to(rows_a[i : i + 1], (8, 128))

    def moment_b(chunk):
        rows = pl.ds(pl.multiple_of(chunk * 24, 8), 24)
        total = jnp.zeros((3, 8, 128), F32)
        for q in range(4):
            some = along[8 * q : 8 * q + 8, rows, :].reshape(8, 3, 8, 128)
            total = total + jnp.sum(some * ua_rows[8 * q : 8 * q + 8][:, None], axis=0)
        return total.reshape(24, 128)

    mb_copies = []
    for peer in xc_peers:
        mb_part[peer[0]] = moment_b(peer[0])
        mb_copies.append(start_one(peer, mb_part.at[peer[0]], mb_slots.at[xc_me]))
    ua_copies = start(gx_peers, ua_slots.at[gx], ua_slots.at[gx])
    moment = moment_b(xc_me)
    drain(22)
    mb_sum[zh_me] = add(moment, mb_copies, xc_peers, mb_slots)
    mb_copies = start(zh_peers, mb_sum.at[zh_me], mb_sum.at[zh_me])
    arrive(ua_copies)
    gram_ua = gram_packed(ua_slots[...].reshape(256, 128))
    scale_a, scale_a_down = scale_rows(gram_ua, float(span_i * 16))
    gram_a = gram_ua / (scale_a * scale_a_down)
    inverse_b = block_diagonal(inverse(gram_a * gram_c))
    unscale_a = 1.0 / scale_a
    moment = add(mb_sum[zh_me], mb_copies, zh_peers, mb_sum)
    ub[xc_me] = matmul(moment * unscale_a, inverse_b)
    ub_copies = start(xc_peers, ub.at[xc_me], ub.at[xc_me])
    shard_a = ua_slots[gx] / scale_a
    full_a = expand(shard_a)
    turned = jnp.concatenate([full_a, full_a, full_a, full_a], axis=0).T
    for i in range(32):
        a_columns[i] = jnp.broadcast_to(turned[:RANK, i : i + 1], (RANK, 128))
    rows_out[:16, :] = jnp.where(gy == 0, shard_a, swap(shard_a))
    out_ref[:4, :] = rows_out[pl.ds(gz * 4, 4), :]
    drain(7)
    arrivals = list(zip(ub_copies, xc_peers, xc_shifts))
    moment = jnp.zeros((RANK, 128), F32)
    for near in (True, False):
        for copy, peer, shift in reversed(arrivals):
            if (shift[0] in (0, 1)) == near:
                copy.wait_recv()
        ends = [x, lax.rem(x + 3, 4)] if near else [lax.rem(x + 1, 4), lax.rem(x + 2, 4)]
        own = [ub[pl.ds(2 * end, 2)].reshape(48, 128) for end in ends]
        turned_high, turned_low = split(jnp.concatenate(own, axis=0).T)
        left = jnp.concatenate(
            [
                jnp.concatenate([turned_high[:RANK], turned_high[RANK:]], axis=1),
                jnp.concatenate([turned_low[:RANK], turned_low[RANK:]], axis=1),
            ],
            axis=0,
        )

        def rows_of(ref, i):
            return jnp.concatenate(
                [
                    ref[i, pl.ds(pl.multiple_of(h * half_j + end * 48, 16), 48), :]
                    for h in range(2)
                    for end in ends
                ],
                axis=0,
            )

        for i in range(0, span_i, 2):
            high = jnp.concatenate([rows_of(thi, i), rows_of(thi, i + 1)], axis=1)
            rest = jnp.concatenate([rows_of(tlo, i), rows_of(tlo, i + 1)], axis=1)
            part = jnp.dot(left, high, preferred_element_type=F32)
            part = part[:RANK] + (part[RANK:] + jnp.dot(left[:RANK], rest, preferred_element_type=F32))
            moment = moment + (part[:, :128] * a_columns[i] + part[:, 128:] * a_columns[i + 1])
    block_b = ub[...].reshape(half_j, 128)
    moment = compact(jnp.concatenate([moment, moment], axis=0).T)
    upper = lax.broadcasted_iota(jnp.int32, (8, 128), 0) < 4
    parts = [[], []]
    for m in range(4):
        one, two = moment[16 * m : 16 * m + 8], moment[16 * m + 8 : 16 * m + 16]
        parts[0].append(jnp.where(upper, one, pltpu.roll(two, 4, 0)))
        parts[1].append(jnp.where(upper, pltpu.roll(one, 4, 0), two))
    parts = [jnp.concatenate(part, axis=0) for part in parts]
    mc_part[...] = jnp.where(gy == 0, parts[1], parts[0])
    mc_copies = start(gy_peers, mc_part, mc_slot)
    gu_slots[gy] = compact(gram_packed(block_b))
    gu_copies = start(gy_peers, gu_slots.at[gy], gu_slots.at[gy])
    drain(2)
    arrive(mc_copies)
    mc_sum[gx] = jnp.where(gy == 0, parts[0], parts[1]) + mc_slot[...]
    mc_copies = start(gx_peers, mc_sum.at[gx], mc_sum.at[gx])
    arrive(gu_copies)
    gram_ub = expand(gu_slots[0] + gu_slots[1])
    scale_b, scale_b_down = scale_rows(gram_ub, float(half_j * 4))
    gram_b = gram_ub / (scale_b * scale_b_down)
    inverse_c = block_diagonal(inverse(gram_a * gram_b))
    unscale_b = 1.0 / scale_b
    shard_b = block_b / scale_b
    b_packed[:half_j, :] = jnp.where(z // 2 == 0, shard_b, swap(shard_b))
    first = lax.rem(z, 2) * 96 + x * 24 + yh * 12 + core * 6
    out_ref[8:14, :] = b_packed[pl.ds(first, 6), :]
    drain(15)
    moment = add(mc_sum[gx], mc_copies, gx_peers, mc_sum)
    uc = matmul(moment * unscale_b, inverse_c)
    ss_slots[yc_me] = fold(jnp.sum(uc * uc, axis=0, keepdims=True))
    ss_copies = start(yc_peers, ss_slots.at[yc_me], ss_slots.at[yc_me])
    rows_out[:32, :] = jnp.where(z // 2 == 0, uc, swap(uc))
    own = rows_out[pl.ds(lax.rem(gx, 8) * 4, 4), :]
    drain(7)
    total = add(ss_slots[yc_me], ss_copies, yc_peers, ss_slots)
    out_ref[4:8, :] = own / jnp.sqrt(total / float(128 * 4) + 1e-06)
    drain()


COPIES = 1 + 3 + 15 + 15 + 3 + 1 + 7 + 7 + 15 + 7 + 7 + 1 + 1 + 15 + 7


def local(tensor, factor_b, factor_c):
    span_i, span_j, span_k = tensor.shape
    half_j = span_j // 2
    vmem = pl.BlockSpec(memory_space=pltpu.VMEM)
    scratch = [
        pltpu.VMEM(tensor.shape, F32),
        pltpu.VMEM(tensor.shape, BF16),
        pltpu.VMEM(tensor.shape, BF16),
        pltpu.VMEM((span_i, half_j, 128), F32),
        pltpu.VMEM((256, 256), BF16),
        pltpu.VMEM((2, 8, RANK), F32),
        pltpu.VMEM((16, 8, 128), F32),
        pltpu.VMEM((4, 8, RANK), F32),
        pltpu.VMEM((17, 12, 128), F32),
        pltpu.VMEM((half_j + 8, 128), F32),
        pltpu.VMEM((2, 32, 128), F32),
        pltpu.VMEM((4, 32, 128), F32),
        pltpu.VMEM((span_i, 8, 128), F32),
        pltpu.VMEM((8, 16, 128), F32),
        pltpu.VMEM((16, 16, 128), F32),
        pltpu.VMEM((32, 8, 128), F32),
        pltpu.VMEM((32, RANK, 128), F32),
        pltpu.VMEM((8, 24, 128), F32),
        pltpu.VMEM((8, 24, 128), F32),
        pltpu.VMEM((8, 24, 128), F32),
        pltpu.VMEM((8, 24, 128), F32),
        pltpu.VMEM((2, 32, 128), F32),
        pltpu.VMEM((32, 128), F32),
        pltpu.VMEM((32, 128), F32),
        pltpu.VMEM((16, 32, 128), F32),
        pltpu.VMEM((16, 1, 128), F32),
        pltpu.VMEM((40, 128), F32),
        pltpu.SemaphoreType.DMA((span_i // GROUP,)),
        pltpu.SemaphoreType.DMA((COPIES,)),
        pltpu.SemaphoreType.DMA((COPIES,)),
        pltpu.SemaphoreType.REGULAR,
    ]
    start = jnp.concatenate(
        [jnp.pad(factor_b, ((0, 2), (0, 0))), jnp.pad(factor_c, ((0, 4), (0, 0)))], axis=0
    )
    out = pl.pallas_call(
        kernel,
        out_shape=jax.ShapeDtypeStruct((16, 128), F32),
        in_specs=[pl.BlockSpec(memory_space=pl.ANY), vmem],
        out_specs=vmem,
        scratch_shapes=scratch,
        compiler_params=pltpu.CompilerParams(
            collective_id=0, has_side_effects=True, vmem_limit_bytes=48 * 1024 * 1024
        ),
    )(tensor, start)
    return out[:4, :RANK], out[8:14, :RANK], out[4:8, :RANK]


def solution(mesh):
    return jax.shard_map(
        local,
        mesh=mesh,
        in_specs=(P("gx", "gy", "gz"), P(("gy", "gx", "gz"), None), P(("gz", "gx", "gy"), None)),
        out_specs=(
            P(("gx", "gy", "gz"), None),
            P(("gy", "gx", "gz"), None),
            P(("gz", "gx", "gy"), None),
        ),
        check_vma=False,
    )
```
